256 devices in a mesh: pulse: 32 (over z_lo, x, core), range: 8 (over y, z_hi).
Axes of the slice: x: 4, y: 4, z: 8 (z_hi: 2, z_lo: 4; z = z_hi * 4 + z_lo), core: 2. Of those that a mesh axis runs over, the one named last changes fastest.
Arguments:
- subimages: bfloat16 [32, 256, 2, 8192], P('pulse', None, None, 'range'), may hold values from -6 to 6
- taps: float32 [32, 3, 256, 4], replicated, may hold values from -3 to 3
- tap_offsets: int32 [32, 3, 256], replicated, may hold values from 0 to 5
- rates: float32 [32, 3, 256], replicated, may hold values from -40 to 40
- phases: float32 [32, 3, 256], replicated, may hold values from -3.140625 to 3.140625
- band_values: bfloat16 [3, 2, 512, 16], replicated, may hold values from -1 to 1
- band_starts: int32 [3, 2, 512], replicated, may hold values from 0 to 240
Outputs:
- merged: bfloat16 [32, 256, 2, 8192], P('pulse', None, None, 'range')
The draws below stay inside these ranges and needn't reach their ends.
All inputs are finite; a program needn't handle non-finite values.
Results may differ from the reference program's by a relative error of at most 0.0076.
Values may be sent and summed in bfloat16 or wider, within the bound.
A program may use at most 64 MiB of HBM per device.

```python
import jax
import jax.numpy as jnp
from jax import lax

A = 256
BAND = 16
TAPS = 4
H = 4
SECTIONS = 3
SUBS = 32
NR = 8192


def plant(drawn, key, least, top_value):
    index_at = [jax.random.randint(jax.random.fold_in(key, axis), (), 0, length) for axis, length in enumerate(drawn.shape)]
    main_axis = drawn.shape.index(max(drawn.shape))
    beside = index_at[:main_axis] + [(index_at[main_axis] + 1) % drawn.shape[main_axis]] + index_at[main_axis + 1:]
    return drawn.at[tuple(index_at)].set(least).at[tuple(beside)].set(top_value)


def level_of(rng, dims, pieces, smallest, high):
    def one(dim, parts):
        draws = jax.random.uniform(jax.random.fold_in(jax.random.fold_in(rng, 6), dim), (parts,), jnp.float32, smallest / len(pieces), high / len(pieces))
        return jnp.repeat(jnp.exp(draws), dims[dim] // parts).reshape((-1,) + (1,) * (len(dims) - dim - 1))

    gain = one(*pieces[0])
    for cut in pieces[1:]:
        gain = gain * one(*cut)
    return gain


def noise(own_key, shape, spread, reach, cuts=(), held_as=jnp.bfloat16):
    gain = level_of(own_key, shape, cuts, -0.22, 0.18) if cuts else 1.0
    values = jax.random.normal(own_key, shape, jnp.float32) * spread * gain
    return jnp.minimum(jnp.maximum(values, -reach), reach).astype(held_as)


def setup_inputs(seed: int = 0) -> dict:
    streams_of = jax.random.split(jax.random.key(seed), 8)
    subimages = noise(streams_of[0], (SUBS, A, 2, NR), 1.0, 6.0, ((0, 32), (3, 8)))
    taps = noise(streams_of[1], (SUBS, SECTIONS, A, TAPS), 0.5, 3.0, (), jnp.float32)
    tap_offsets = plant(jax.random.randint(streams_of[2], (SUBS, SECTIONS, A), 0, 2 * H - TAPS + 2), jax.random.fold_in(streams_of[2], 1), 0, (2 * H - TAPS + 2) - 1).astype(jnp.int32)
    rates = jnp.clip(jax.random.uniform(streams_of[3], (SUBS, SECTIONS, A), jnp.float32, -40.0, 40.0), -40.0, 40.0)
    phases = jnp.clip(jax.random.uniform(streams_of[4], (SUBS, SECTIONS, A), jnp.float32, -3.140625, 3.140625), -3.140625, 3.140625)
    band_values = noise(streams_of[5], (SECTIONS, 2, 2 * A, BAND), (2 * BAND) ** -0.5, 1.0)
    band_starts = plant(jax.random.randint(streams_of[6], (SECTIONS, 2, 2 * A), 0, A - BAND + 1), jax.random.fold_in(streams_of[6], 1), 0, A - BAND).astype(jnp.int32)
    return {"subimages": subimages, "taps": taps, "tap_offsets": tap_offsets, "rates": rates, "phases": phases, "band_values": band_values, "band_starts": band_starts}


def spread_taps(tap_row, offset_row, width):
    shifts = jnp.arange(width, dtype=jnp.int32)[None, :] - offset_row[:, None]
    weights = jnp.zeros((tap_row.shape[0], width), jnp.float32)
    for tap_index in range(tap_row.shape[1]):
        weights = weights + jnp.where(shifts == tap_index, tap_row[:, tap_index:tap_index + 1].astype(jnp.float32), 0.0)
    return weights


def interpolate(padded, weights, rate_row, phase_row, first_bin, swath_bins):
    width = weights.shape[1]
    bins = padded.shape[-1] - (width - 1)
    accum = jnp.zeros((padded.shape[0], 2, bins), jnp.float32)
    for shift in range(width):
        accum = accum + weights[:, shift, None, None] * padded[:, :, shift:shift + bins].astype(jnp.float32)
    positions = (first_bin + jnp.arange(bins, dtype=jnp.int32)).astype(jnp.float32)
    angle = phase_row[:, None] + rate_row[:, None] * (positions[None, :] + 0.5) / swath_bins
    cosine = jnp.cos(angle)
    sine = jnp.sin(angle)
    real_part = accum[:, 0] * cosine - accum[:, 1] * sine
    imag_part = accum[:, 0] * sine + accum[:, 1] * cosine
    return jnp.stack([real_part, imag_part], axis=1).astype(jnp.bfloat16)


def reference(subimages, taps, tap_offsets, rates, phases, band_values, band_starts):
    current = subimages
    subs = current.shape[0]
    beams = current.shape[1]
    swath_bins = current.shape[3]
    width = 2 * H + 1
    for section in range(SECTIONS):
        stride = 2 ** section
        padded = jnp.pad(current, ((0, 0), (0, 0), (0, 0), (H, H)))

        def turn_one(index_sub):
            weights = spread_taps(taps[index_sub, section], tap_offsets[index_sub, section], width)
            return interpolate(padded[index_sub], weights, rates[index_sub, section], phases[index_sub, section], 0, swath_bins)

        turned = lax.map(turn_one, jnp.arange(subs, dtype=jnp.int32))

        def merge_one(index_sub):
            side_bit = (index_sub >> section) & 1
            low_index = index_sub - side_bit * stride
            first_row = side_bit * beams
            accum = jnp.zeros((beams, 2, swath_bins), jnp.float32)
            for child in range(2):
                source = turned[low_index + child * stride]
                values = lax.dynamic_slice(band_values[section, child], (first_row, jnp.int32(0)), (beams, BAND)).astype(jnp.float32)
                starts = lax.dynamic_slice(band_starts[section, child], (first_row,), (beams,))
                for column in range(BAND):
                    rows = jnp.take(source, (starts + column).astype(jnp.int32), axis=0).astype(jnp.float32)
                    accum = accum + values[:, column, None, None] * rows
            return accum.astype(jnp.bfloat16)

        current = lax.map(merge_one, jnp.arange(subs, dtype=jnp.int32))
    return current
```

```python
import functools

import jax
import jax.numpy as jnp
from jax import lax
from jax.experimental import pallas as pl
from jax.experimental.pallas import tpu as pltpu
from jax.sharding import PartitionSpec as P

MESH = pl.DeviceIdType.MESH
F32 = jnp.float32
BF16 = jnp.bfloat16

BEAMS = 256
BAND = 16
TAPS = 4
WIDTH = 9
GROUP = 8
BINS = 1024
BLOCK = BINS // GROUP
EDGE = 16
SENT = BLOCK + 16
TURNED = BINS + 16

TURN0 = ((0, 96), (96, 48))
TURN1 = ((0, 80), (80, 64))
TURN2 = ((0, 64), (64, 64))


def nt_dot(left, right):
    return lax.dot_general(left, right, (((1,), (1,)), ((), ())), preferred_element_type=F32)


def identity(size):
    rows = lax.broadcasted_iota(jnp.int32, (size, size), 0)
    columns = lax.broadcasted_iota(jnp.int32, (size, size), 1)
    return jnp.where(rows == columns, 1.0, 0.0).astype(BF16)


def flip(index, bits):
    return sum(lax.rem(index // bit + bits // bit, 2) * bit for bit in (1, 2, 4))


def spread(taps, offset):
    shifts = lax.broadcasted_iota(jnp.int32, (16, BEAMS), 0) - offset
    weights = jnp.zeros((16, BEAMS), F32)
    for tap in range(TAPS):
        weights = weights + jnp.where(shifts == tap, taps[tap : tap + 1, :], 0.0)
    return weights


def phasor_tables(rate, phase, first_bin, tiles, swath):
    first = first_bin + 16 * lax.broadcasted_iota(jnp.int32, (tiles, BEAMS), 0)
    coarse = phase + rate * (first.astype(F32) + 0.5) / swath
    fine = rate * lax.broadcasted_iota(jnp.int32, (16, BEAMS), 0).astype(F32) / swath
    return jnp.cos(coarse), jnp.sin(coarse), jnp.cos(fine), jnp.sin(fine)


def turn_tile(load, weights, coarse, fine):
    real = load(0, 0) * weights[0]
    imag = load(1, 0) * weights[0]
    for shift in range(1, WIDTH):
        real = real + load(0, shift) * weights[shift]
        imag = imag + load(1, shift) * weights[shift]
    cosine = coarse[0] * fine[0] - coarse[1] * fine[1]
    sine = coarse[1] * fine[0] + coarse[0] * fine[1]
    return real * cosine - imag * sine, real * sine + imag * cosine


def kernel(
    ranges,
    x_ref, taps_ref, offsets_ref, rates_ref, phases_ref, values_ref, starts_ref,
    out_ref,
    raw, edge_out, edge_in, turned0, got0, image1, turned1, image2, turned2, done, got,
    matrices, weights, coarse, fine, coarse0, rates, phases, offsets,
    edge_send, edge_recv, in_send, in_recv, out_send, out_recv, own_sem,
):
    pulse = lax.axis_index("pulse")
    rng = lax.axis_index("range")
    me = lax.rem(pulse, GROUP)
    base = pulse - me
    swath = float(BINS * ranges)
    after, before = lax.rem(rng + 1, ranges), lax.rem(rng + ranges - 1, ranges)
    peers = [flip(me, k) for k in range(GROUP)]

    barrier = pltpu.get_barrier_semaphore()
    for k in range(1, GROUP):
        pl.semaphore_signal(barrier, 1, device_id=(base + peers[k], rng), device_id_type=MESH)
    for other in (after, before):
        pl.semaphore_signal(barrier, 1, device_id=(pulse, other), device_id_type=MESH)

    eye = identity(BLOCK)
    for block in range(GROUP):
        for part in range(2):
            raw[part, EDGE + block * BLOCK : EDGE + (block + 1) * BLOCK, :] = nt_dot(
                eye, x_ref[part, :, block * BLOCK : (block + 1) * BLOCK]
            )
    for part in range(2):
        edge_out[0, part] = raw[part, BINS : BINS + EDGE, :].astype(BF16)
        edge_out[1, part] = raw[part, EDGE : 2 * EDGE, :].astype(BF16)

    def edge_copy(side):
        return pltpu.make_async_remote_copy(
            src_ref=edge_out.at[side],
            dst_ref=edge_in.at[side],
            send_sem=edge_send.at[side],
            recv_sem=edge_recv.at[side],
            device_id=(pulse, after if side == 0 else before),
            device_id_type=MESH,
        )

    pl.semaphore_wait(barrier, GROUP + 1)
    edge_copy(0).start()
    edge_copy(1).start()

    rows8 = pl.ds(pl.multiple_of(base, 8), 8)
    for section in range(3):
        for ref, kept in ((rates_ref, rates), (phases_ref, phases), (offsets_ref, offsets)):
            group = ref[section, rows8, :]
            for sub in range(GROUP):
                kept[section, sub] = jnp.broadcast_to(group[sub : sub + 1, :], (8, BEAMS))

    weights[0, 0] = spread(taps_ref[pulse, 0], offsets[0, me, 0:1, :])
    tables = phasor_tables(rates[0, me, 0:1, :], phases[0, me, 0:1, :], rng * BINS - 8, 72, swath)
    coarse0[0], coarse0[1] = tables[0], tables[1]
    fine[0, 0, 0], fine[0, 0, 1] = tables[2], tables[3]

    def turn_own(near, tiles, far, first):
        for half in range(2):
            lanes = slice(half * 128, half * 128 + 128)
            taps = [weights[0, 0, j : j + 1, lanes] for j in range(WIDTH)]
            close = [fine[0, 0, c, :, lanes] for c in range(2)]
            for tile in range(tiles):

                def load(part, shift):
                    return near[part, 16 * tile + 4 + shift : 16 * tile + 20 + shift, lanes]

                real, imag = turn_tile(
                    load, taps, [far[c][tile : tile + 1, lanes] for c in range(2)], close
                )
                rows = pl.ds(pl.multiple_of(first + 16 * tile, 16), 16)
                turned0[0, rows, lanes] = real.astype(BF16)
                turned0[1, rows, lanes] = imag.astype(BF16)

    def in_copy(chunk, k, peer):
        first, rows = TURN0[chunk]
        return pltpu.make_async_remote_copy(
            src_ref=turned0.at[:, pl.ds(pl.multiple_of(peer * BLOCK + first, 16), rows), :],
            dst_ref=got0.at[lax.rem(me, 2), me // 2, :, pl.ds(first, rows), :],
            send_sem=in_send.at[chunk, k],
            recv_sem=in_recv.at[chunk, k],
            device_id=(base + peer, rng),
            device_id_type=MESH,
        )

    def own_in_copy(chunk):
        first, rows = TURN0[chunk]
        return pltpu.make_async_copy(
            turned0.at[:, pl.ds(pl.multiple_of(me * BLOCK + first, 16), rows), :],
            got0.at[lax.rem(me, 2), me // 2, :, pl.ds(first, rows), :],
            own_sem.at[chunk],
        )

    def turn_block(block):
        first = pl.multiple_of(block * BLOCK, BLOCK)
        turn_own(
            raw.at[:, pl.ds(first, BLOCK + 16), :],
            BLOCK // 16,
            [coarse0[c, pl.ds(pl.multiple_of(block * 8, 8), 8), :] for c in range(2)],
            first,
        )

    def turn_and_send(i, carry):
        k = GROUP - 1 - i
        peer = flip(me, k)
        turn_block(peer)

        @pl.when(jnp.logical_and(peer != 0, k != 0))
        def _():
            in_copy(0, k, peer).start()

        return carry

    lax.fori_loop(0, GROUP, turn_and_send, 0)

    def build(section):
        for child in range(2):
            starts = starts_ref[section, child : child + 1, :]

            def step(i, carry):
                first = pl.multiple_of(i * 32, 32)
                gaps = lax.broadcasted_iota(jnp.int32, (32, 2 * BEAMS), 0) + first - starts
                values = values_ref[section, child].astype(F32)
                dense = jnp.zeros((32, 2 * BEAMS), F32)
                for column in range(BAND):
                    dense = jnp.where(gaps == column, values[column : column + 1, :], dense)
                rows = pl.ds(pl.multiple_of(first + child * BEAMS, 32), 32)
                matrices[section, rows, :] = dense.astype(BF16)
                return carry

            lax.fori_loop(0, 8, step, 0)

    def prepare(section, first_bin):
        def step(sub, carry):
            weights[section, sub] = spread(
                taps_ref[base + sub, section], offsets[section, sub, 0:1, :]
            )
            tables = phasor_tables(
                rates[section, sub, 0:1, :], phases[section, sub, 0:1, :], first_bin, 16, swath
            )
            for c in range(2):
                coarse[section - 1, sub, c] = tables[c]
                fine[section, sub, c] = tables[2 + c]
            return carry

        lax.fori_loop(0, GROUP, step, 0)

    build(0)

    edge_copy(0).wait()
    edge_copy(1).wait()
    for part in range(2):
        raw[part, 0:EDGE, :] = jnp.where(rng == 0, 0.0, edge_in[0, part].astype(F32))
        raw[part, BINS + EDGE : BINS + 2 * EDGE, :] = jnp.where(
            rng == ranges - 1, 0.0, edge_in[1, part].astype(F32)
        )
    for tile in (0, TURNED // 16 - 1):
        turn_own(
            raw.at[:, tile * 16 : tile * 16 + 32, :],
            1,
            [coarse0[c, tile : tile + 1, :] for c in range(2)],
            tile * 16,
        )

    @pl.when(me != 0)
    def _():
        in_copy(0, me, 0).start()

    own_in_copy(0).start()
    for k in (4, 2, 6, 5, 3, 7, 1):
        in_copy(1, k, peers[k]).start()
    own_in_copy(1).start()

    first_bin = rng * BINS + me * BLOCK
    prepare(1, first_bin - 4)
    build(1)
    prepare(2, first_bin)
    build(2)

    def merge(section, turned, first, rows):
        left = jnp.concatenate(
            [turned[k, :, :, first : first + rows, :].reshape(GROUP * rows, BEAMS) for k in range(2)],
            axis=1,
        )
        return jnp.dot(left, matrices[section], preferred_element_type=F32)

    def place(section, group, side):
        low = group % 2 ** section
        return (group - low) * 2 + side * 2 ** section + low

    def keep(section, product, image, first, rows):
        for group in range(4):
            for side in range(2):
                image[place(section, group, side), :, first : first + rows, :] = product[
                    group * 2 * rows : (group + 1) * 2 * rows, side * BEAMS : (side + 1) * BEAMS
                ].reshape(2, rows, BEAMS)

    def turn(section, image, turned, first, rows):
        def step(sub, carry):
            child = lax.rem(sub // 2 ** section, 2)
            low = lax.rem(sub, 2 ** section)
            group = sub // 2 ** (section + 1) * 2 ** section + low
            for half in range(2):
                lanes = slice(half * 128, half * 128 + 128)
                taps = [weights[section, sub, j : j + 1, lanes] for j in range(WIDTH)]
                near = [fine[section, sub, c, :, lanes] for c in range(2)]
                for row in range(first, first + rows, 16):

                    def load(part, shift):
                        return image[sub, part, row + shift : row + shift + 16, lanes]

                    tile = row // 16
                    real, imag = turn_tile(
                        load,
                        taps,
                        [coarse[section - 1, sub, c, tile : tile + 1, lanes] for c in range(2)],
                        near,
                    )
                    turned[child, group, 0, row : row + 16, lanes] = real.astype(BF16)
                    turned[child, group, 1, row : row + 16, lanes] = imag.astype(BF16)
            return carry

        lax.fori_loop(0, GROUP, step, 0)

    def out_copy(chunk, k):
        return pltpu.make_async_remote_copy(
            src_ref=done.at[chunk, peers[k]],
            dst_ref=got.at[:, pl.ds(pl.multiple_of(me * BLOCK + chunk * 64, 16), 64), :],
            send_sem=out_send.at[chunk, k],
            recv_sem=out_recv.at[chunk, k],
            device_id=(base + peers[k], rng),
            device_id_type=MESH,
        )

    def own_out_copy(chunk):
        return pltpu.make_async_copy(
            done.at[chunk, me],
            got.at[:, pl.ds(pl.multiple_of(me * BLOCK + chunk * 64, 16), 64), :],
            own_sem.at[2 + chunk],
        )

    low_end = jnp.logical_and(rng == 0, me == 0)
    high_end = jnp.logical_and(rng == ranges - 1, me == GROUP - 1)
    image1[:, :, SENT : SENT + 8, :] = jnp.zeros((GROUP, 2, 8, BEAMS), F32)

    for chunk in range(2):
        for k in range(1, GROUP):
            in_copy(chunk, k, peers[k]).wait_recv()
        own_in_copy(chunk).wait()
        first, rows = TURN0[chunk]
        keep(0, merge(0, got0, first, rows), image1, first, rows)
        if chunk == 0:

            @pl.when(low_end)
            def _():
                image1[:, :, 0:8, :] = jnp.zeros((GROUP, 2, 8, BEAMS), F32)

        else:

            @pl.when(high_end)
            def _():
                image1[:, :, SENT - 8 : SENT, :] = jnp.zeros((GROUP, 2, 8, BEAMS), F32)

        first, rows = TURN1[chunk]
        turn(1, image1, turned1, first, rows)
        keep(1, merge(1, turned1, first, rows), image2, first, rows)
        if chunk == 0:

            @pl.when(low_end)
            def _():
                image2[:, :, 0:4, :] = jnp.zeros((GROUP, 2, 4, BEAMS), F32)

        else:

            @pl.when(high_end)
            def _():
                image2[:, :, BLOCK + 4 : BLOCK + 8, :] = jnp.zeros((GROUP, 2, 4, BEAMS), F32)

        first, rows = TURN2[chunk]
        turn(2, image2, turned2, first, rows)
        product = merge(2, turned2, first, rows)
        for group in range(4):
            for side in range(2):
                done[chunk, place(2, group, side)] = (
                    product[
                        group * 2 * rows : (group + 1) * 2 * rows,
                        side * BEAMS : (side + 1) * BEAMS,
                    ]
                    .reshape(2, rows, BEAMS)
                    .astype(BF16)
                )
        for k in (4, 2, 6, 5, 3, 7, 1):
            out_copy(chunk, k).start()
        own_out_copy(chunk).start()

    wide_eye = identity(BEAMS)
    for k in (0, 1, 2, 3, 4, 5, 6, 7):
        if k == 0:
            own_out_copy(0).wait()
            own_out_copy(1).wait()
        else:
            out_copy(0, k).wait_recv()
            out_copy(1, k).wait_recv()
        start = pl.multiple_of(peers[k] * BLOCK, BLOCK)
        for part in range(2):
            out_ref[part, :, pl.ds(start, BLOCK)] = nt_dot(
                wide_eye, got[part, pl.ds(start, BLOCK), :]
            ).astype(BF16)

    for chunk in range(2):
        for k in range(1, GROUP):
            in_copy(chunk, k, peers[k]).wait_send()
            out_copy(chunk, k).wait_send()


def body(subimages, taps, tap_offsets, rates, phases, band_values, band_starts):
    ranges = lax.axis_size("range")
    whole = pl.BlockSpec(memory_space=pltpu.VMEM)
    merged = pl.pallas_call(
        functools.partial(kernel, ranges),
        out_shape=jax.ShapeDtypeStruct((2, BEAMS, BINS), BF16),
        in_specs=[whole] * 7,
        out_specs=whole,
        scratch_shapes=[
            pltpu.VMEM((2, BINS + 2 * EDGE, BEAMS), F32),
            pltpu.VMEM((2, 2, EDGE, BEAMS), BF16),
            pltpu.VMEM((2, 2, EDGE, BEAMS), BF16),
            pltpu.VMEM((2, TURNED, BEAMS), BF16),
            pltpu.VMEM((2, 4, 2, SENT, BEAMS), BF16),
            pltpu.VMEM((GROUP, 2, SENT + 8, BEAMS), F32),
            pltpu.VMEM((2, 4, 2, SENT, BEAMS), BF16),
            pltpu.VMEM((GROUP, 2, SENT, BEAMS), F32),
            pltpu.VMEM((2, 4, 2, BLOCK, BEAMS), BF16),
            pltpu.VMEM((2, GROUP, 2, BLOCK // 2, BEAMS), BF16),
            pltpu.VMEM((2, BINS, BEAMS), BF16),
            pltpu.VMEM((3, 2 * BEAMS, 2 * BEAMS), BF16),
            pltpu.VMEM((3, GROUP, 16, BEAMS), F32),
            pltpu.VMEM((2, GROUP, 2, 16, BEAMS), F32),
            pltpu.VMEM((3, GROUP, 2, 16, BEAMS), F32),
            pltpu.VMEM((2, 72, BEAMS), F32),
            pltpu.VMEM((3, GROUP, 8, BEAMS), F32),
            pltpu.VMEM((3, GROUP, 8, BEAMS), F32),
            pltpu.VMEM((3, GROUP, 8, BEAMS), jnp.int32),
            pltpu.SemaphoreType.DMA((2,)),
            pltpu.SemaphoreType.DMA((2,)),
            pltpu.SemaphoreType.DMA((2, GROUP)),
            pltpu.SemaphoreType.DMA((2, GROUP)),
            pltpu.SemaphoreType.DMA((2, GROUP)),
            pltpu.SemaphoreType.DMA((2, GROUP)),
            pltpu.SemaphoreType.DMA((4,)),
        ],
        compiler_params=pltpu.CompilerParams(
            collective_id=0, has_side_effects=True, vmem_limit_bytes=50 * 2 ** 20
        ),
    )(
        jnp.transpose(subimages[0], (1, 0, 2)),
        jnp.transpose(taps, (0, 1, 3, 2)),
        jnp.transpose(tap_offsets, (1, 0, 2)),
        jnp.transpose(rates, (1, 0, 2)),
        jnp.transpose(phases, (1, 0, 2)),
        jnp.transpose(band_values, (0, 1, 3, 2)),
        band_starts,
    )
    return jnp.transpose(merged, (1, 0, 2))[None]


def solution(mesh):
    placed = (P("pulse", None, None, "range"), P(), P(), P(), P(), P(), P())
    return jax.shard_map(
        body, mesh=mesh, in_specs=placed, out_specs=P("pulse", None, None, "range"), check_vma=False
    )
```

```python
import functools

import jax
import jax.numpy as jnp
from jax import lax
from jax.experimental import pallas as pl
from jax.experimental.pallas import tpu as pltpu
from jax.sharding import PartitionSpec as P

MESH = pl.DeviceIdType.MESH
F32 = jnp.float32
BF16 = jnp.bfloat16

BEAMS = 256
BAND = 16
TAPS = 4
WIDTH = 9
GROUP = 8
BINS = 1024
BLOCK = BINS // GROUP
EDGE = 16
SENT = BLOCK + 16
TURNED = BINS + 16

TURN0 = ((0, 96), (96, 48))
TURN1 = ((0, 80), (80, 64))
TURN2 = ((0, 64), (64, 64))

CHUNK_0, CHUNK_1, HEAD, REST = (0, 96, 0), (96, 48, 1), (0, 16, 2), (16, 80, 0)


def nt_dot(left, right):
    return lax.dot_general(left, right, (((1,), (1,)), ((), ())), preferred_element_type=F32)


def identity(size):
    rows = lax.broadcasted_iota(jnp.int32, (size, size), 0)
    columns = lax.broadcasted_iota(jnp.int32, (size, size), 1)
    return jnp.where(rows == columns, 1.0, 0.0).astype(BF16)


def flip(index, bits):
    return sum(lax.rem(index // bit + bits // bit, 2) * bit for bit in (1, 2, 4))


def spread(taps, offset):
    shifts = lax.broadcasted_iota(jnp.int32, (16, BEAMS), 0) - offset
    weights = jnp.zeros((16, BEAMS), F32)
    for tap in range(TAPS):
        weights = weights + jnp.where(shifts == tap, taps[tap : tap + 1, :], 0.0)
    return weights


def times(a, b):
    return a[0] * b[0] - a[1] * b[1], a[1] * b[0] + a[0] * b[1]


def unit(angle):
    return jnp.cos(angle), jnp.sin(angle)


def ladder(first, step):
    rows = lax.broadcasted_iota(jnp.int32, (8, BEAMS), 0)
    low = first
    for bit in (1, 2, 4):
        taken = jnp.bitwise_and(rows, bit) != 0
        low = times(low, (jnp.where(taken, step[0], 1.0), jnp.where(taken, step[1], 0.0)))
        step = times(step, step)
    return low, times(low, step)


def row_of(pair, row):
    return tuple(jnp.broadcast_to(value[row : row + 1, :], (8, BEAMS)) for value in pair)


def turn_tile(load, weights, coarse, fine):
    real = load(0, 0) * weights[0]
    imag = load(1, 0) * weights[0]
    for shift in range(1, WIDTH):
        real = real + load(0, shift) * weights[shift]
        imag = imag + load(1, shift) * weights[shift]
    cosine = coarse[0] * fine[0] - coarse[1] * fine[1]
    sine = coarse[1] * fine[0] + coarse[0] * fine[1]
    return real * cosine - imag * sine, real * sine + imag * cosine


def kernel(
    ranges,
    x_ref, taps_ref, offsets_ref, rates_ref, phases_ref, values_ref, starts_ref,
    out_ref,
    raw, edge_out, edge_in, turned0, got0, image1, turned1, image2, turned2, done, got,
    matrices, weights, coarse, fine, coarse0,
    edge_send, edge_recv, in_send, in_recv, out_send, out_recv, own_sem,
):
    pulse = lax.axis_index("pulse")
    rng = lax.axis_index("range")
    me = lax.rem(pulse, GROUP)
    base = pulse - me
    swath = float(BINS * ranges)
    after, before = lax.rem(rng + 1, ranges), lax.rem(rng + ranges - 1, ranges)
    peers = [flip(me, k) for k in range(GROUP)]

    barrier = pltpu.get_barrier_semaphore()
    for k in range(1, GROUP):
        pl.semaphore_signal(barrier, 1, device_id=(base + peers[k], rng), device_id_type=MESH)
    for other in (after, before):
        pl.semaphore_signal(barrier, 1, device_id=(pulse, other), device_id_type=MESH)

    eye = identity(BLOCK)
    for block in range(GROUP):
        for part in range(2):
            rows = nt_dot(eye, x_ref[part, :, block * BLOCK : (block + 1) * BLOCK])
            for half in range(2):
                raw[part, half, EDGE + block * BLOCK : EDGE + (block + 1) * BLOCK, :] = rows[
                    :, half * 128 : half * 128 + 128
                ]
    for part in range(2):
        for half in range(2):
            lanes = slice(half * 128, half * 128 + 128)
            edge_out[0, part, :, lanes] = raw[part, half, BINS : BINS + EDGE, :].astype(BF16)
            edge_out[1, part, :, lanes] = raw[part, half, EDGE : 2 * EDGE, :].astype(BF16)

    def edge_copy(side):
        return pltpu.make_async_remote_copy(
            src_ref=edge_out.at[side],
            dst_ref=edge_in.at[side],
            send_sem=edge_send.at[side],
            recv_sem=edge_recv.at[side],
            device_id=(pulse, after if side == 0 else before),
            device_id_type=MESH,
        )

    pl.semaphore_wait(barrier, GROUP + 1)
    edge_copy(0).start()
    edge_copy(1).start()

    rows8 = pl.ds(pl.multiple_of(base, 8), 8)
    mine = lax.broadcasted_iota(jnp.int32, (8, BEAMS), 0) == me

    def own(ref):
        value = jnp.sum(jnp.where(mine, ref[0, rows8, :], 0), axis=0, keepdims=True)
        return jnp.broadcast_to(value, (8, BEAMS))

    weights[0, 0] = spread(taps_ref[pulse, 0], own(offsets_ref)[0:1, :])
    rate, phase = own(rates_ref) / swath, own(phases_ref)
    nothing = jnp.ones_like(rate), jnp.zeros_like(rate)
    close = ladder(nothing, unit(rate))
    tiles = ladder(unit(phase + rate * ((rng * BINS - 8).astype(F32) + 0.5)), unit(rate * 16.0))
    blocks = ladder(nothing, unit(rate * 128.0))
    for block in range(GROUP + 1):
        far = times(tiles[0], row_of(blocks[block // 8], block % 8))
        coarse0[block, 0], coarse0[block, 1] = far
    for c in range(2):
        fine[0, 0, c, 0:8], fine[0, 0, c, 8:16] = close[0][c], close[1][c]

    def turn_own(near, tiles, far, first):
        for half in range(2):
            lanes = slice(half * 128, half * 128 + 128)
            taps = [weights[0, 0, j : j + 1, lanes] for j in range(WIDTH)]
            close = [fine[0, 0, c, :, lanes] for c in range(2)]
            for tile in range(tiles):

                def load(part, shift):
                    return near[part, half, 16 * tile + 4 + shift : 16 * tile + 20 + shift, :]

                real, imag = turn_tile(
                    load, taps, [far[c][tile : tile + 1, lanes] for c in range(2)], close
                )
                rows = pl.ds(pl.multiple_of(first + 16 * tile, 16), 16)
                turned0[0, rows, lanes] = real.astype(BF16)
                turned0[1, rows, lanes] = imag.astype(BF16)

    def in_copy(piece, k, peer):
        first, rows, sem = piece
        return pltpu.make_async_remote_copy(
            src_ref=turned0.at[:, pl.ds(pl.multiple_of(peer * BLOCK + first, 16), rows), :],
            dst_ref=got0.at[lax.rem(me, 2), me // 2, :, pl.ds(first, rows), :],
            send_sem=in_send.at[sem, k],
            recv_sem=in_recv.at[sem, k],
            device_id=(base + peer, rng),
            device_id_type=MESH,
        )

    def own_in_copy(chunk):
        first, rows = TURN0[chunk]
        return pltpu.make_async_copy(
            turned0.at[:, pl.ds(pl.multiple_of(me * BLOCK + first, 16), rows), :],
            got0.at[lax.rem(me, 2), me // 2, :, pl.ds(first, rows), :],
            own_sem.at[chunk],
        )

    def turn_block(block):
        first = pl.multiple_of(block * BLOCK, BLOCK)
        turn_own(
            raw.at[:, :, pl.ds(first, BLOCK + 16), :],
            BLOCK // 16,
            [coarse0[block, c] for c in range(2)],
            first,
        )

    def turn_and_send(i, carry):
        k = GROUP - 1 - i
        peer = flip(me, k)
        turn_block(peer)

        @pl.when(jnp.logical_and(peer != 0, k != 0))
        def _():
            in_copy(CHUNK_0, k, peer).start()

        @pl.when(jnp.logical_and(peer == 0, k != 0))
        def _():
            in_copy(REST, k, peer).start()

        return carry

    lax.fori_loop(0, GROUP, turn_and_send, 0)

    def build(section):
        rows = lax.broadcasted_iota(jnp.int32, (BAND, 2 * BEAMS), 0)
        for child in range(2):
            starts = starts_ref[section, child : child + 1, :]
            shift = jnp.bitwise_and(starts, BAND - 1)
            band = values_ref[section, child].astype(F32)
            for bit in (1, 2, 4, 8):
                rolled = jnp.concatenate([band[BAND - bit :], band[: BAND - bit]], axis=0)
                band = jnp.where(jnp.bitwise_and(shift, bit) != 0, rolled, band)
            home = starts - shift + jnp.where(rows < shift, BAND, 0)
            for first in range(0, BEAMS, BAND):
                matrices[section, child * BEAMS + first : child * BEAMS + first + BAND, :] = (
                    jnp.where(home == first, band, 0.0).astype(BF16)
                )

    def prepare(section, first_bin):
        rate, phase = rates_ref[section, rows8, :] / swath, phases_ref[section, rows8, :]
        offsets = offsets_ref[section, rows8, :]
        start = unit(phase + rate * (first_bin.astype(F32) + 0.5))
        short, long = unit(rate), unit(rate * 16.0)
        for sub in range(GROUP):
            weights[section, sub] = spread(taps_ref[base + sub, section], offsets[sub : sub + 1, :])
            near = ladder(nothing, row_of(short, sub))
            far = ladder(row_of(start, sub), row_of(long, sub))
            for c in range(2):
                for half in range(2):
                    fine[section, sub, c, half * 8 : half * 8 + 8] = near[half][c]
                    coarse[section - 1, sub, c, half * 8 : half * 8 + 8] = far[half][c]

    first_bin = rng * BINS + me * BLOCK
    build(0)
    prepare(1, first_bin - 4)
    build(1)
    prepare(2, first_bin)
    build(2)

    edge_copy(0).wait()
    edge_copy(1).wait()
    for part in range(2):
        for half in range(2):
            lanes = slice(half * 128, half * 128 + 128)
            raw[part, half, 0:EDGE, :] = jnp.where(
                rng == 0, 0.0, edge_in[0, part, :, lanes].astype(F32)
            )
            raw[part, half, BINS + EDGE : BINS + 2 * EDGE, :] = jnp.where(
                rng == ranges - 1, 0.0, edge_in[1, part, :, lanes].astype(F32)
            )
    for tile in (0, TURNED // 16 - 1):
        turn_own(
            raw.at[:, :, tile * 16 : tile * 16 + 32, :],
            1,
            [coarse0[tile // 8, c] for c in range(2)],
            tile * 16,
        )

    @pl.when(me != 0)
    def _():
        in_copy(HEAD, me, 0).start()

    own_in_copy(0).start()
    for k in (4, 2, 6, 5, 3, 7, 1):
        in_copy(CHUNK_1, k, peers[k]).start()
    own_in_copy(1).start()

    def merge(section, turned, first, rows):
        left = jnp.concatenate(
            [turned[k, :, :, first : first + rows, :].reshape(GROUP * rows, BEAMS) for k in range(2)],
            axis=1,
        )
        return jnp.dot(left, matrices[section], preferred_element_type=F32)

    def place(section, group, side):
        low = group % 2 ** section
        return (group - low) * 2 + side * 2 ** section + low

    def keep(section, product, image, first, rows):
        for group in range(4):
            for side in range(2):
                for half in range(2):
                    lanes = slice(side * BEAMS + half * 128, side * BEAMS + half * 128 + 128)
                    image[place(section, group, side), :, half, first : first + rows, :] = product[
                        group * 2 * rows : (group + 1) * 2 * rows, lanes
                    ].reshape(2, rows, 128)

    def turn(section, image, turned, first, rows):
        def step(sub, carry):
            child = lax.rem(sub // 2 ** section, 2)
            low = lax.rem(sub, 2 ** section)
            group = sub // 2 ** (section + 1) * 2 ** section + low
            for half in range(2):
                lanes = slice(half * 128, half * 128 + 128)
                taps = [weights[section, sub, j : j + 1, lanes] for j in range(WIDTH)]
                near = [fine[section, sub, c, :, lanes] for c in range(2)]
                for row in range(first, first + rows, 16):

                    def load(part, shift):
                        return image[sub, part, half, row + shift : row + shift + 16, :]

                    tile = row // 16
                    real, imag = turn_tile(
                        load,
                        taps,
                        [coarse[section - 1, sub, c, tile : tile + 1, lanes] for c in range(2)],
                        near,
                    )
                    turned[child, group, 0, row : row + 16, lanes] = real.astype(BF16)
                    turned[child, group, 1, row : row + 16, lanes] = imag.astype(BF16)
            return carry

        lax.fori_loop(0, GROUP, step, 0)

    def out_copy(chunk, k):
        return pltpu.make_async_remote_copy(
            src_ref=done.at[chunk, peers[k]],
            dst_ref=got.at[:, pl.ds(pl.multiple_of(me * BLOCK + chunk * 64, 16), 64), :],
            send_sem=out_send.at[chunk, k],
            recv_sem=out_recv.at[chunk, k],
            device_id=(base + peers[k], rng),
            device_id_type=MESH,
        )

    def own_out_copy(chunk):
        return pltpu.make_async_copy(
            done.at[chunk, me],
            got.at[:, pl.ds(pl.multiple_of(me * BLOCK + chunk * 64, 16), 64), :],
            own_sem.at[2 + chunk],
        )

    low_end = jnp.logical_and(rng == 0, me == 0)
    high_end = jnp.logical_and(rng == ranges - 1, me == GROUP - 1)
    image1[:, :, :, SENT : SENT + 8, :] = jnp.zeros((GROUP, 2, 2, 8, 128), F32)

    for chunk in range(2):
        if chunk == 0:

            @pl.when(me != 0)
            def _():
                for k in range(1, GROUP):
                    in_copy(CHUNK_0, k, peers[k]).wait_recv()

            @pl.when(me == 0)
            def _():
                for k in range(1, GROUP):
                    in_copy(REST, k, peers[k]).wait_recv()
                    in_copy(HEAD, k, peers[k]).wait_recv()

        else:
            for k in range(1, GROUP):
                in_copy(CHUNK_1, k, peers[k]).wait_recv()
        own_in_copy(chunk).wait()
        first, rows = TURN0[chunk]
        keep(0, merge(0, got0, first, rows), image1, first, rows)
        if chunk == 0:

            @pl.when(low_end)
            def _():
                image1[:, :, :, 0:8, :] = jnp.zeros((GROUP, 2, 2, 8, 128), F32)

        else:

            @pl.when(high_end)
            def _():
                image1[:, :, :, SENT - 8 : SENT, :] = jnp.zeros((GROUP, 2, 2, 8, 128), F32)

        first, rows = TURN1[chunk]
        turn(1, image1, turned1, first, rows)
        keep(1, merge(1, turned1, first, rows), image2, first, rows)
        if chunk == 0:

            @pl.when(low_end)
            def _():
                image2[:, :, :, 0:4, :] = jnp.zeros((GROUP, 2, 2, 4, 128), F32)

        else:

            @pl.when(high_end)
            def _():
                image2[:, :, :, BLOCK + 4 : BLOCK + 8, :] = jnp.zeros((GROUP, 2, 2, 4, 128), F32)

        first, rows = TURN2[chunk]
        turn(2, image2, turned2, first, rows)
        product = merge(2, turned2, first, rows)
        for group in range(4):
            for side in range(2):
                done[chunk, place(2, group, side)] = (
                    product[
                        group * 2 * rows : (group + 1) * 2 * rows,
                        side * BEAMS : (side + 1) * BEAMS,
                    ]
                    .reshape(2, rows, BEAMS)
                    .astype(BF16)
                )
        for k in (4, 2, 6, 5, 3, 7, 1):
            out_copy(chunk, k).start()
        own_out_copy(chunk).start()

    wide_eye = identity(BEAMS)
    for k in (0, 1, 2, 3, 4, 5, 6, 7):
        if k == 0:
            own_out_copy(0).wait()
            own_out_copy(1).wait()
        else:
            out_copy(0, k).wait_recv()
            out_copy(1, k).wait_recv()
        start = pl.multiple_of(peers[k] * BLOCK, BLOCK)
        for part in range(2):
            out_ref[part, :, pl.ds(start, BLOCK)] = nt_dot(
                wide_eye, got[part, pl.ds(start, BLOCK), :]
            ).astype(BF16)

    for k in range(1, GROUP):

        @pl.when(peers[k] != 0)
        def _():
            in_copy(CHUNK_0, k, peers[k]).wait_send()

        @pl.when(peers[k] == 0)
        def _():
            in_copy(REST, k, peers[k]).wait_send()
            in_copy(HEAD, k, peers[k]).wait_send()

        in_copy(CHUNK_1, k, peers[k]).wait_send()
        out_copy(0, k).wait_send()
        out_copy(1, k).wait_send()


def body(subimages, taps, tap_offsets, rates, phases, band_values, band_starts):
    ranges = lax.axis_size("range")
    whole = pl.BlockSpec(memory_space=pltpu.VMEM)
    merged = pl.pallas_call(
        functools.partial(kernel, ranges),
        out_shape=jax.ShapeDtypeStruct((2, BEAMS, BINS), BF16),
        in_specs=[whole] * 7,
        out_specs=whole,
        scratch_shapes=[
            pltpu.VMEM((2, 2, BINS + 2 * EDGE, 128), F32),
            pltpu.VMEM((2, 2, EDGE, BEAMS), BF16),
            pltpu.VMEM((2, 2, EDGE, BEAMS), BF16),
            pltpu.VMEM((2, TURNED, BEAMS), BF16),
            pltpu.VMEM((2, 4, 2, SENT, BEAMS), BF16),
            pltpu.VMEM((GROUP, 2, 2, SENT + 8, 128), F32),
            pltpu.VMEM((2, 4, 2, SENT, BEAMS), BF16),
            pltpu.VMEM((GROUP, 2, 2, SENT, 128), F32),
            pltpu.VMEM((2, 4, 2, BLOCK, BEAMS), BF16),
            pltpu.VMEM((2, GROUP, 2, BLOCK // 2, BEAMS), BF16),
            pltpu.VMEM((2, BINS, BEAMS), BF16),
            pltpu.VMEM((3, 2 * BEAMS, 2 * BEAMS), BF16),
            pltpu.VMEM((3, GROUP, 16, BEAMS), F32),
            pltpu.VMEM((2, GROUP, 2, 16, BEAMS), F32),
            pltpu.VMEM((3, GROUP, 2, 16, BEAMS), F32),
            pltpu.VMEM((GROUP + 1, 2, 8, BEAMS), F32),
            pltpu.SemaphoreType.DMA((2,)),
            pltpu.SemaphoreType.DMA((2,)),
            pltpu.SemaphoreType.DMA((3, GROUP)),
            pltpu.SemaphoreType.DMA((3, GROUP)),
            pltpu.SemaphoreType.DMA((2, GROUP)),
            pltpu.SemaphoreType.DMA((2, GROUP)),
            pltpu.SemaphoreType.DMA((4,)),
        ],
        compiler_params=pltpu.CompilerParams(
            collective_id=0, has_side_effects=True, vmem_limit_bytes=50 * 2 ** 20
        ),
    )(
        jnp.transpose(subimages[0], (1, 0, 2)),
        jnp.transpose(taps, (0, 1, 3, 2)),
        jnp.transpose(tap_offsets, (1, 0, 2)),
        jnp.transpose(rates, (1, 0, 2)),
        jnp.transpose(phases, (1, 0, 2)),
        jnp.transpose(band_values, (0, 1, 3, 2)),
        band_starts,
    )
    return jnp.transpose(merged, (1, 0, 2))[None]


def solution(mesh):
    placed = (P("pulse", None, None, "range"), P(), P(), P(), P(), P(), P())
    return jax.shard_map(
        body, mesh=mesh, in_specs=placed, out_specs=P("pulse", None, None, "range"), check_vma=False
    )
```

```python
import functools

import jax
import jax.numpy as jnp
from jax import lax
from jax.experimental import pallas as pl
from jax.experimental.pallas import tpu as pltpu
from jax.sharding import PartitionSpec as P

MESH = pl.DeviceIdType.MESH
F32 = jnp.float32
BF16 = jnp.bfloat16

BEAMS = 256
BAND = 16
TAPS = 4
WIDTH = 9
GROUP = 8
BINS = 1024
BLOCK = BINS // GROUP
EDGE = 16
SENT = BLOCK + 16
TURNED = BINS + 16

TURN0, TURN1, TURN2 = (96, 48), (80, 64), (64, 64)
UPPER0, UPPER1, UPPER2 = (48, 96), (64, 80), (64, 64)


def nt_dot(left, right):
    return lax.dot_general(left, right, (((1,), (1,)), ((), ())), preferred_element_type=F32)


def identity(size):
    rows = lax.broadcasted_iota(jnp.int32, (size, size), 0)
    columns = lax.broadcasted_iota(jnp.int32, (size, size), 1)
    return jnp.where(rows == columns, 1.0, 0.0).astype(BF16)


def flip(index, bits):
    return sum(lax.rem(index // bit + bits // bit, 2) * bit for bit in (1, 2, 4))


def spread(taps, offset):
    shifts = lax.broadcasted_iota(jnp.int32, (16, BEAMS), 0) - offset
    weights = jnp.zeros((16, BEAMS), F32)
    for tap in range(TAPS):
        weights = weights + jnp.where(shifts == tap, taps[tap : tap + 1, :], 0.0)
    return weights


def times(a, b):
    return a[0] * b[0] - a[1] * b[1], a[1] * b[0] + a[0] * b[1]


def unit(angle):
    return jnp.cos(angle), jnp.sin(angle)


def ladder(first, step):
    rows = lax.broadcasted_iota(jnp.int32, (8, BEAMS), 0)
    low = first
    for bit in (1, 2, 4):
        taken = jnp.bitwise_and(rows, bit) != 0
        low = times(low, (jnp.where(taken, step[0], 1.0), jnp.where(taken, step[1], 0.0)))
        step = times(step, step)
    return low, times(low, step)


def row_of(pair, row):
    return tuple(jnp.broadcast_to(value[row : row + 1, :], (8, BEAMS)) for value in pair)


def turn_tile(load, weights, coarse, fine):
    real = load(0, 0) * weights[0]
    imag = load(1, 0) * weights[0]
    for shift in range(1, WIDTH):
        real = real + load(0, shift) * weights[shift]
        imag = imag + load(1, shift) * weights[shift]
    cosine = coarse[0] * fine[0] - coarse[1] * fine[1]
    sine = coarse[1] * fine[0] + coarse[0] * fine[1]
    return real * cosine - imag * sine, real * sine + imag * cosine


def kernel(
    ranges,
    x_ref, taps_ref, offsets_ref, rates_ref, phases_ref, values_ref, starts_ref,
    out_ref,
    raw, edge_out, edge_in, turned0, got0, image1, turned1, image2, turned2, done, got,
    matrices, weights, coarse, fine, coarse0,
    credit, edge_send, edge_recv, in_send, in_recv, out_send, out_recv, own_sem,
):
    pulse = lax.axis_index("pulse")
    rng = lax.axis_index("range")
    me = lax.rem(pulse, GROUP)
    base = pulse - me
    swath = float(BINS * ranges)
    after, before = lax.rem(rng + 1, ranges), lax.rem(rng + ranges - 1, ranges)
    peers = [flip(me, k) for k in range(GROUP)]

    even = lax.rem(rng, 2) == 0
    has_before, has_after = rng > 0, rng < ranges - 1

    def place_of(chunk, upper, device):
        flipped = 1 - jnp.minimum(device, 1)
        return pl.multiple_of(upper[chunk] * (flipped if chunk == 0 else 1 - flipped), 16)

    barrier = pltpu.get_barrier_semaphore()
    for k in range(1, GROUP):
        pl.semaphore_signal(barrier, 1, device_id=(base + peers[k], rng), device_id_type=MESH)

    @pl.when(jnp.logical_and(even, has_after))
    def _():
        pl.semaphore_signal(barrier, 1, device_id=(pulse, after), device_id_type=MESH)

    @pl.when(jnp.logical_and(even, has_before))
    def _():
        pl.semaphore_signal(barrier, 1, device_id=(pulse, before), device_id_type=MESH)

    eye = identity(BLOCK)
    for block in range(GROUP):
        for part in range(2):
            rows = nt_dot(eye, x_ref[part, :, block * BLOCK : (block + 1) * BLOCK])
            for half in range(2):
                raw[part, half, EDGE + block * BLOCK : EDGE + (block + 1) * BLOCK, :] = rows[
                    :, half * 128 : half * 128 + 128
                ]
    for part in range(2):
        for half in range(2):
            lanes = slice(half * 128, half * 128 + 128)
            edge_out[0, part, :, lanes] = raw[part, half, BINS : BINS + EDGE, :].astype(BF16)
            edge_out[1, part, :, lanes] = raw[part, half, EDGE : 2 * EDGE, :].astype(BF16)

    def edge_copy(side):
        return pltpu.make_async_remote_copy(
            src_ref=edge_out.at[side],
            dst_ref=edge_in.at[side],
            send_sem=edge_send.at[side],
            recv_sem=edge_recv.at[side],
            device_id=(pulse, after if side == 0 else before),
            device_id_type=MESH,
        )

    @pl.when(even)
    def _():
        pl.semaphore_wait(barrier, GROUP - 1)

    @pl.when(jnp.logical_not(even))
    def _():
        pl.semaphore_wait(barrier, GROUP + jnp.where(has_after, 1, 0))
        pl.semaphore_signal(
            credit.at[0], 1, device_id=(pulse, before), device_id_type=MESH
        )
        edge_copy(1).start()

        @pl.when(has_after)
        def _():
            pl.semaphore_signal(
                credit.at[1], 1, device_id=(pulse, after), device_id_type=MESH
            )
            edge_copy(0).start()

    rows8 = pl.ds(pl.multiple_of(base, 8), 8)
    mine = lax.broadcasted_iota(jnp.int32, (8, BEAMS), 0) == me

    def own(ref):
        value = jnp.sum(jnp.where(mine, ref[0, rows8, :], 0), axis=0, keepdims=True)
        return jnp.broadcast_to(value, (8, BEAMS))

    weights[0, 0] = spread(taps_ref[pulse, 0], own(offsets_ref)[0:1, :])
    rate, phase = own(rates_ref) / swath, own(phases_ref)
    nothing = jnp.ones_like(rate), jnp.zeros_like(rate)
    close = ladder(nothing, unit(rate))
    tiles = ladder(unit(phase + rate * ((rng * BINS - 8).astype(F32) + 0.5)), unit(rate * 16.0))
    blocks = ladder(nothing, unit(rate * 128.0))
    for block in range(GROUP + 1):
        far = times(tiles[0], row_of(blocks[block // 8], block % 8))
        coarse0[block, 0], coarse0[block, 1] = far
    for c in range(2):
        fine[0, 0, c, 0:8], fine[0, 0, c, 8:16] = close[0][c], close[1][c]

    def turn_own(near, tiles, far, first):
        for half in range(2):
            lanes = slice(half * 128, half * 128 + 128)
            taps = [weights[0, 0, j : j + 1, lanes] for j in range(WIDTH)]
            close = [fine[0, 0, c, :, lanes] for c in range(2)]
            for tile in range(tiles):

                def load(part, shift):
                    return near[part, half, 16 * tile + 4 + shift : 16 * tile + 20 + shift, :]

                real, imag = turn_tile(
                    load, taps, [far[c][tile : tile + 1, lanes] for c in range(2)], close
                )
                rows = pl.ds(pl.multiple_of(first + 16 * tile, 16), 16)
                turned0[0, rows, lanes] = real.astype(BF16)
                turned0[1, rows, lanes] = imag.astype(BF16)

    def in_rows(chunk, device):
        return place_of(chunk, UPPER0, device), TURN0[chunk]

    def in_copy(chunk, k, peer):
        first, rows = in_rows(chunk, peer)
        return pltpu.make_async_remote_copy(
            src_ref=turned0.at[:, pl.ds(pl.multiple_of(peer * BLOCK + first, 16), rows), :],
            dst_ref=got0.at[lax.rem(me, 2), me // 2, :, pl.ds(first, rows), :],
            send_sem=in_send.at[chunk, k],
            recv_sem=in_recv.at[chunk, k],
            device_id=(base + peer, rng),
            device_id_type=MESH,
        )

    def own_in_copy(chunk):
        first, rows = in_rows(chunk, me)
        return pltpu.make_async_copy(
            turned0.at[:, pl.ds(pl.multiple_of(me * BLOCK + first, 16), rows), :],
            got0.at[lax.rem(me, 2), me // 2, :, pl.ds(first, rows), :],
            own_sem.at[chunk],
        )

    def turn_block(block):
        first = pl.multiple_of(block * BLOCK, BLOCK)
        turn_own(
            raw.at[:, :, pl.ds(first, BLOCK + 16), :],
            BLOCK // 16,
            [coarse0[block, c] for c in range(2)],
            first,
        )

    order = (4, 2, 6, 5, 3, 7, 1)

    def turn_and_send(i, carry):
        k = GROUP - 1 - i
        peer = flip(me, k)
        turn_block(peer)

        @pl.when(jnp.logical_and(peer != 0, k != 0))
        def _():
            in_copy(0, k, peer).start()

        return carry

    lax.fori_loop(0, GROUP, turn_and_send, 0)

    @pl.when(me != 0)
    def _():
        in_copy(0, me, 0).start()

    own_in_copy(0).start()

    def inner(peer):
        return jnp.logical_and(peer > 0, peer < GROUP - 1)

    for k in order:

        @pl.when(inner(peers[k]))
        def _():
            in_copy(1, k, peers[k]).start()

    def build(section):
        rows = lax.broadcasted_iota(jnp.int32, (BAND, 2 * BEAMS), 0)
        for child in range(2):
            starts = starts_ref[section, child : child + 1, :]
            shift = jnp.bitwise_and(starts, BAND - 1)
            band = values_ref[section, child].astype(F32)
            for bit in (1, 2, 4, 8):
                rolled = jnp.concatenate([band[BAND - bit :], band[: BAND - bit]], axis=0)
                band = jnp.where(jnp.bitwise_and(shift, bit) != 0, rolled, band)
            home = starts - shift + jnp.where(rows < shift, BAND, 0)
            for first in range(0, BEAMS, BAND):
                matrices[section, child * BEAMS + first : child * BEAMS + first + BAND, :] = (
                    jnp.where(home == first, band, 0.0).astype(BF16)
                )

    def prepare(section, first_bin):
        rate, phase = rates_ref[section, rows8, :] / swath, phases_ref[section, rows8, :]
        offsets = offsets_ref[section, rows8, :]
        upper = (UPPER1, UPPER2)[section - 1]
        starts = [
            unit(phase + rate * ((first_bin + place_of(chunk, upper, me)).astype(F32) + 0.5))
            for chunk in range(2)
        ]
        short, long = unit(rate), unit(rate * 16.0)
        for sub in range(GROUP):
            weights[section, sub] = spread(taps_ref[base + sub, section], offsets[sub : sub + 1, :])
            near = ladder(nothing, row_of(short, sub))
            for c in range(2):
                for half in range(2):
                    fine[section, sub, c, half * 8 : half * 8 + 8] = near[half][c]
            for chunk in range(2):
                far = ladder(row_of(starts[chunk], sub), row_of(long, sub))[0]
                coarse[section - 1, sub, chunk, 0], coarse[section - 1, sub, chunk, 1] = far

    first_bin = rng * BINS + me * BLOCK
    build(0)
    prepare(1, first_bin - 4)
    build(1)
    prepare(2, first_bin)
    build(2)

    @pl.when(jnp.logical_and(even, has_after))
    def _():
        pl.semaphore_wait(credit.at[0], 1)
        edge_copy(0).start()

    @pl.when(jnp.logical_and(even, has_before))
    def _():
        pl.semaphore_wait(credit.at[1], 1)
        edge_copy(1).start()

    for side, there, first in ((0, has_before, 0), (1, has_after, BINS + EDGE)):

        @pl.when(there)
        def _():
            edge_copy(side).wait_recv()
            for part in range(2):
                for half in range(2):
                    raw[part, half, first : first + EDGE, :] = edge_in[
                        side, part, :, half * 128 : half * 128 + 128
                    ].astype(F32)

        @pl.when(jnp.logical_not(there))
        def _():
            raw[:, :, first : first + EDGE, :] = jnp.zeros((2, 2, EDGE, 128), F32)

    for tile in (0, TURNED // 16 - 1):
        turn_own(
            raw.at[:, :, tile * 16 : tile * 16 + 32, :],
            1,
            [coarse0[tile // 8, c] for c in range(2)],
            tile * 16,
        )

    for k in order:

        @pl.when(jnp.logical_not(inner(peers[k])))
        def _():
            in_copy(1, k, peers[k]).start()

    own_in_copy(1).start()

    def merge(section, turned, first, rows):
        left = jnp.concatenate(
            [turned[k, :, :, pl.ds(first, rows), :].reshape(GROUP * rows, BEAMS) for k in range(2)],
            axis=1,
        )
        return jnp.dot(left, matrices[section], preferred_element_type=F32)

    def place(section, group, side):
        low = group % 2 ** section
        return (group - low) * 2 + side * 2 ** section + low

    def keep(section, product, image, first, rows):
        for group in range(4):
            for side in range(2):
                for half in range(2):
                    lanes = slice(side * BEAMS + half * 128, side * BEAMS + half * 128 + 128)
                    image[place(section, group, side), :, half, pl.ds(first, rows), :] = product[
                        group * 2 * rows : (group + 1) * 2 * rows, lanes
                    ].reshape(2, rows, 128)

    def turn(section, chunk, image, turned, first, rows):
        def step(sub, carry):
            child = lax.rem(sub // 2 ** section, 2)
            low = lax.rem(sub, 2 ** section)
            group = sub // 2 ** (section + 1) * 2 ** section + low
            for half in range(2):
                lanes = slice(half * 128, half * 128 + 128)
                taps = [weights[section, sub, j : j + 1, lanes] for j in range(WIDTH)]
                near = [fine[section, sub, c, :, lanes] for c in range(2)]
                source = image.at[sub, :, half, pl.ds(first, rows + 8), :]
                for row in range(0, rows, 16):

                    def load(part, shift):
                        return source[part, row + shift : row + shift + 16, :]

                    tile = row // 16
                    real, imag = turn_tile(
                        load,
                        taps,
                        [
                            coarse[section - 1, sub, chunk, c, tile : tile + 1, lanes]
                            for c in range(2)
                        ],
                        near,
                    )
                    target = pl.ds(pl.multiple_of(first + row, 16), 16)
                    turned[child, group, 0, target, lanes] = real.astype(BF16)
                    turned[child, group, 1, target, lanes] = imag.astype(BF16)
            return carry

        lax.fori_loop(0, GROUP, step, 0)

    def out_rows(chunk):
        return pl.ds(pl.multiple_of(me * BLOCK + place_of(chunk, UPPER2, me), 16), TURN2[chunk])

    def out_copy(chunk, k):
        return pltpu.make_async_remote_copy(
            src_ref=done.at[chunk, peers[k]],
            dst_ref=got.at[:, out_rows(chunk), :],
            send_sem=out_send.at[chunk, k],
            recv_sem=out_recv.at[chunk, k],
            device_id=(base + peers[k], rng),
            device_id_type=MESH,
        )

    def own_out_copy(chunk):
        return pltpu.make_async_copy(
            done.at[chunk, me], got.at[:, out_rows(chunk), :], own_sem.at[2 + chunk]
        )

    low_end = jnp.logical_and(rng == 0, me == 0)
    high_end = jnp.logical_and(rng == ranges - 1, me == GROUP - 1)
    image1[:, :, :, SENT : SENT + 8, :] = jnp.zeros((GROUP, 2, 2, 8, 128), F32)

    for chunk in range(2):
        for k in range(1, GROUP):
            in_copy(chunk, k, me).wait_recv()
        own_in_copy(chunk).wait()
        first, rows = in_rows(chunk, me)
        keep(0, merge(0, got0, first, rows), image1, first, rows)
        if chunk == 1:

            @pl.when(low_end)
            def _():
                image1[:, :, :, 0:8, :] = jnp.zeros((GROUP, 2, 2, 8, 128), F32)

            @pl.when(high_end)
            def _():
                image1[:, :, :, SENT - 8 : SENT, :] = jnp.zeros((GROUP, 2, 2, 8, 128), F32)

        first, rows = place_of(chunk, UPPER1, me), TURN1[chunk]
        turn(1, chunk, image1, turned1, first, rows)
        keep(1, merge(1, turned1, first, rows), image2, first, rows)
        if chunk == 1:

            @pl.when(low_end)
            def _():
                image2[:, :, :, 0:4, :] = jnp.zeros((GROUP, 2, 2, 4, 128), F32)

            @pl.when(high_end)
            def _():
                image2[:, :, :, BLOCK + 4 : BLOCK + 8, :] = jnp.zeros((GROUP, 2, 2, 4, 128), F32)

        first, rows = place_of(chunk, UPPER2, me), TURN2[chunk]
        turn(2, chunk, image2, turned2, first, rows)
        product = merge(2, turned2, first, rows)
        for group in range(4):
            for side in range(2):
                done[chunk, place(2, group, side)] = (
                    product[
                        group * 2 * rows : (group + 1) * 2 * rows,
                        side * BEAMS : (side + 1) * BEAMS,
                    ]
                    .reshape(2, rows, BEAMS)
                    .astype(BF16)
                )
        for k in order:
            out_copy(chunk, k).start()
        own_out_copy(chunk).start()

    wide_eye = identity(BEAMS)
    for k in (0, 1, 2, 3, 4, 5, 6, 7):
        if k == 0:
            own_out_copy(0).wait()
            own_out_copy(1).wait()
        else:
            out_copy(0, k).wait_recv()
            out_copy(1, k).wait_recv()
        start = pl.multiple_of(peers[k] * BLOCK, BLOCK)
        for part in range(2):
            out_ref[part, :, pl.ds(start, BLOCK)] = nt_dot(
                wide_eye, got[part, pl.ds(start, BLOCK), :]
            ).astype(BF16)

    for k in range(1, GROUP):
        for chunk in range(2):
            in_copy(chunk, k, peers[k]).wait_send()
            out_copy(chunk, k).wait_send()

    @pl.when(has_after)
    def _():
        edge_copy(0).wait_send()

    @pl.when(has_before)
    def _():
        edge_copy(1).wait_send()


def body(subimages, taps, tap_offsets, rates, phases, band_values, band_starts):
    ranges = lax.axis_size("range")
    whole = pl.BlockSpec(memory_space=pltpu.VMEM)
    merged = pl.pallas_call(
        functools.partial(kernel, ranges),
        out_shape=jax.ShapeDtypeStruct((2, BEAMS, BINS), BF16),
        in_specs=[whole] * 7,
        out_specs=whole,
        scratch_shapes=[
            pltpu.VMEM((2, 2, BINS + 2 * EDGE, 128), F32),
            pltpu.VMEM((2, 2, EDGE, BEAMS), BF16),
            pltpu.VMEM((2, 2, EDGE, BEAMS), BF16),
            pltpu.VMEM((2, TURNED, BEAMS), BF16),
            pltpu.VMEM((2, 4, 2, SENT, BEAMS), BF16),
            pltpu.VMEM((GROUP, 2, 2, SENT + 8, 128), F32),
            pltpu.VMEM((2, 4, 2, SENT, BEAMS), BF16),
            pltpu.VMEM((GROUP, 2, 2, SENT, 128), F32),
            pltpu.VMEM((2, 4, 2, BLOCK, BEAMS), BF16),
            pltpu.VMEM((2, GROUP, 2, BLOCK // 2, BEAMS), BF16),
            pltpu.VMEM((2, BINS, BEAMS), BF16),
            pltpu.VMEM((3, 2 * BEAMS, 2 * BEAMS), BF16),
            pltpu.VMEM((3, GROUP, 16, BEAMS), F32),
            pltpu.VMEM((2, GROUP, 2, 2, 8, BEAMS), F32),
            pltpu.VMEM((3, GROUP, 2, 16, BEAMS), F32),
            pltpu.VMEM((GROUP + 1, 2, 8, BEAMS), F32),
            pltpu.SemaphoreType.REGULAR((2,)),
            pltpu.SemaphoreType.DMA((2,)),
            pltpu.SemaphoreType.DMA((2,)),
            pltpu.SemaphoreType.DMA((2, GROUP)),
            pltpu.SemaphoreType.DMA((2, GROUP)),
            pltpu.SemaphoreType.DMA((2, GROUP)),
            pltpu.SemaphoreType.DMA((2, GROUP)),
            pltpu.SemaphoreType.DMA((4,)),
        ],
        compiler_params=pltpu.CompilerParams(
            collective_id=0, has_side_effects=True, vmem_limit_bytes=50 * 2 ** 20
        ),
    )(
        jnp.transpose(subimages[0], (1, 0, 2)),
        jnp.transpose(taps, (0, 1, 3, 2)),
        jnp.transpose(tap_offsets, (1, 0, 2)),
        jnp.transpose(rates, (1, 0, 2)),
        jnp.transpose(phases, (1, 0, 2)),
        jnp.transpose(band_values, (0, 1, 3, 2)),
        band_starts,
    )
    return jnp.transpose(merged, (1, 0, 2))[None]


def solution(mesh):
    placed = (P("pulse", None, None, "range"), P(), P(), P(), P(), P(), P())
    return jax.shard_map(
        body, mesh=mesh, in_specs=placed, out_specs=P("pulse", None, None, "range"), check_vma=False
    )
```

```python
import functools

import jax
import jax.numpy as jnp
from jax import lax
from jax.experimental import pallas as pl
from jax.experimental.pallas import tpu as pltpu
from jax.sharding import PartitionSpec as P

MESH = pl.DeviceIdType.MESH
F32 = jnp.float32
BF16 = jnp.bfloat16

BEAMS = 256
BAND = 16
TAPS = 4
WIDTH = 9
GROUP = 8
BINS = 1024
BLOCK = BINS // GROUP
EDGE = 16
PIECES = 2
PITCH = 17
SENT = BLOCK + 16
TURNED = BINS + 16

TURN0, TURN1, TURN2 = (96, 48), (80, 64), (64, 64)
UPPER0, UPPER1, UPPER2 = (48, 96), (64, 80), (64, 64)


def nt_dot(left, right):
    return lax.dot_general(left, right, (((1,), (1,)), ((), ())), preferred_element_type=F32)


def identity(size):
    rows = lax.broadcasted_iota(jnp.int32, (size, size), 0)
    columns = lax.broadcasted_iota(jnp.int32, (size, size), 1)
    return jnp.where(rows == columns, 1.0, 0.0).astype(BF16)


def flip(index, bits):
    return sum(lax.rem(index // bit + bits // bit, 2) * bit for bit in (1, 2, 4))


def spread(taps, offset):
    shifts = lax.broadcasted_iota(jnp.int32, (16, BEAMS), 0) - offset
    weights = jnp.zeros((16, BEAMS), F32)
    for tap in range(TAPS):
        weights = weights + jnp.where(shifts == tap, taps[tap : tap + 1, :], 0.0)
    return weights


def times(a, b):
    return a[0] * b[0] - a[1] * b[1], a[1] * b[0] + a[0] * b[1]


def unit(angle):
    return jnp.cos(angle), jnp.sin(angle)


def ladder(first, step):
    rows = lax.broadcasted_iota(jnp.int32, (8, BEAMS), 0)
    low = first
    for bit in (1, 2, 4):
        taken = jnp.bitwise_and(rows, bit) != 0
        low = times(low, (jnp.where(taken, step[0], 1.0), jnp.where(taken, step[1], 0.0)))
        step = times(step, step)
    return low, times(low, step)


def row_of(pair, row):
    return tuple(jnp.broadcast_to(value[row : row + 1, :], (8, BEAMS)) for value in pair)


def turn_tile(load, weights, coarse, fine):
    real = load(0, 0) * weights[0]
    imag = load(1, 0) * weights[0]
    for shift in range(1, WIDTH):
        real = real + load(0, shift) * weights[shift]
        imag = imag + load(1, shift) * weights[shift]
    cosine = coarse[0] * fine[0] - coarse[1] * fine[1]
    sine = coarse[1] * fine[0] + coarse[0] * fine[1]
    return real * cosine - imag * sine, real * sine + imag * cosine


def kernel(
    ranges,
    x_hbm, taps_hbm, offsets_hbm, rates_hbm, phases_hbm, values_hbm, starts_hbm,
    got,
    x_ref, taps_ref, offsets_ref, rates_ref, phases_ref, values_ref, starts_ref, spaced, load_sem,
    raw, edge_out, edge_in, turned0, got0, image1, turned1, image2, turned2, done,
    matrices, weights, coarse, fine, coarse0,
    credit, edge_send, edge_recv, in_send, in_recv, out_send, out_recv, own_sem,
):
    pulse = lax.axis_index("pulse")
    rng = lax.axis_index("range")
    me = lax.rem(pulse, GROUP)
    base = pulse - me
    swath = float(BINS * ranges)
    after, before = lax.rem(rng + 1, ranges), lax.rem(rng + ranges - 1, ranges)
    peers = [flip(me, k) for k in range(GROUP)]

    even = lax.rem(rng, 2) == 0
    has_before, has_after = rng > 0, rng < ranges - 1

    def place_of(chunk, upper, device):
        flipped = 1 - jnp.minimum(device, 1)
        return pl.multiple_of(upper[chunk] * (flipped if chunk == 0 else 1 - flipped), 16)

    barrier = pltpu.get_barrier_semaphore()
    for k in range(1, GROUP):
        pl.semaphore_signal(barrier, 1, device_id=(base + peers[k], rng), device_id_type=MESH)

    @pl.when(jnp.logical_and(even, has_after))
    def _():
        pl.semaphore_signal(barrier, 1, device_id=(pulse, after), device_id_type=MESH)

    @pl.when(jnp.logical_and(even, has_before))
    def _():
        pl.semaphore_signal(barrier, 1, device_id=(pulse, before), device_id_type=MESH)

    rows8 = pl.ds(pl.multiple_of(base, GROUP), GROUP)
    loads = [
        pltpu.make_async_copy(source, kept, load_sem.at[i])
        for i, (source, kept) in enumerate(
            (
                (rates_hbm.at[:, rows8, :], rates_ref),
                (phases_hbm.at[:, rows8, :], phases_ref),
                (offsets_hbm.at[:, rows8, :], offsets_ref),
                (taps_hbm.at[rows8], taps_ref),
                (x_hbm, x_ref),
                (values_hbm, values_ref),
                (starts_hbm, starts_ref),
            )
        )
    ]
    for load in loads:
        load.start()
    for load in loads[:4]:
        load.wait()

    mine = lax.broadcasted_iota(jnp.int32, (8, BEAMS), 0) == me

    def own(ref):
        value = jnp.sum(jnp.where(mine, ref[0], 0), axis=0, keepdims=True)
        return jnp.broadcast_to(value, (8, BEAMS))

    weights[0, 0] = spread(taps_ref[me, 0], own(offsets_ref)[0:1, :])
    rate, phase = own(rates_ref) / swath, own(phases_ref)
    nothing = jnp.ones_like(rate), jnp.zeros_like(rate)
    close = ladder(nothing, unit(rate))
    tiles = ladder(unit(phase + rate * ((rng * BINS - 8).astype(F32) + 0.5)), unit(rate * 16.0))
    blocks = ladder(nothing, unit(rate * 128.0))
    for block in range(GROUP + 1):
        far = times(tiles[0], row_of(blocks[block // 8], block % 8))
        coarse0[block, 0], coarse0[block, 1] = far
    for c in range(2):
        fine[0, 0, c, 0:8], fine[0, 0, c, 8:16] = close[0][c], close[1][c]

    eye = identity(BLOCK)
    loads[4].wait()
    for beam in range(BEAMS):
        spaced[PITCH * beam : PITCH * beam + 2 * GROUP, :] = x_ref[beam].astype(F32)
    for block in range(GROUP):
        for part in range(2):
            picked = spaced[pl.ds(2 * block + part, BEAMS, stride=PITCH), :]
            rows = nt_dot(eye, picked.astype(BF16))
            for half in range(2):
                raw[part, half, EDGE + block * BLOCK : EDGE + (block + 1) * BLOCK, :] = rows[
                    :, half * 128 : half * 128 + 128
                ]
    for part in range(2):
        for half in range(2):
            lanes = slice(half * 128, half * 128 + 128)
            edge_out[0, part, :, lanes] = raw[part, half, BINS : BINS + EDGE, :].astype(BF16)
            edge_out[1, part, :, lanes] = raw[part, half, EDGE : 2 * EDGE, :].astype(BF16)

    def edge_copy(side):
        return pltpu.make_async_remote_copy(
            src_ref=edge_out.at[side],
            dst_ref=edge_in.at[side],
            send_sem=edge_send.at[side],
            recv_sem=edge_recv.at[side],
            device_id=(pulse, after if side == 0 else before),
            device_id_type=MESH,
        )

    @pl.when(even)
    def _():
        pl.semaphore_wait(barrier, GROUP - 1)

    @pl.when(jnp.logical_not(even))
    def _():
        pl.semaphore_wait(barrier, GROUP + jnp.where(has_after, 1, 0))
        pl.semaphore_signal(
            credit.at[0], 1, device_id=(pulse, before), device_id_type=MESH
        )
        edge_copy(1).start()

        @pl.when(has_after)
        def _():
            pl.semaphore_signal(
                credit.at[1], 1, device_id=(pulse, after), device_id_type=MESH
            )
            edge_copy(0).start()

    def turn_own(near, tiles, far, first):
        for half in range(2):
            lanes = slice(half * 128, half * 128 + 128)
            taps = [weights[0, 0, j : j + 1, lanes] for j in range(WIDTH)]
            close = [fine[0, 0, c, :, lanes] for c in range(2)]
            for tile in range(tiles):

                def load(part, shift):
                    return near[part, half, 16 * tile + 4 + shift : 16 * tile + 20 + shift, :]

                real, imag = turn_tile(
                    load, taps, [far[c][tile : tile + 1, lanes] for c in range(2)], close
                )
                rows = pl.ds(pl.multiple_of(first + 16 * tile, 16), 16)
                turned0[0, rows, lanes] = real.astype(BF16)
                turned0[1, rows, lanes] = imag.astype(BF16)

    def in_rows(chunk, device):
        return place_of(chunk, UPPER0, device), TURN0[chunk]

    def in_copy(chunk, k, peer):
        first, rows = in_rows(chunk, peer)
        return pltpu.make_async_remote_copy(
            src_ref=turned0.at[:, pl.ds(pl.multiple_of(peer * BLOCK + first, 16), rows), :],
            dst_ref=got0.at[lax.rem(me, 2), me // 2, :, pl.ds(first, rows), :],
            send_sem=in_send.at[chunk, k],
            recv_sem=in_recv.at[chunk, k],
            device_id=(base + peer, rng),
            device_id_type=MESH,
        )

    def own_in_copy(chunk):
        first, rows = in_rows(chunk, me)
        return pltpu.make_async_copy(
            turned0.at[:, pl.ds(pl.multiple_of(me * BLOCK + first, 16), rows), :],
            got0.at[lax.rem(me, 2), me // 2, :, pl.ds(first, rows), :],
            own_sem.at[chunk],
        )

    def turn_block(block):
        first = pl.multiple_of(block * BLOCK, BLOCK)
        turn_own(
            raw.at[:, :, pl.ds(first, BLOCK + 16), :],
            BLOCK // 16,
            [coarse0[block, c] for c in range(2)],
            first,
        )

    order = (4, 2, 6, 5, 3, 7, 1)

    def turn_and_send(i, carry):
        k = GROUP - 1 - i
        peer = flip(me, k)
        turn_block(peer)

        @pl.when(jnp.logical_and(peer != 0, k != 0))
        def _():
            in_copy(0, k, peer).start()

        return carry

    lax.fori_loop(0, GROUP, turn_and_send, 0)

    @pl.when(me != 0)
    def _():
        in_copy(0, me, 0).start()

    own_in_copy(0).start()

    def inner(peer):
        return jnp.logical_and(peer > 0, peer < GROUP - 1)

    for k in order:

        @pl.when(inner(peers[k]))
        def _():
            in_copy(1, k, peers[k]).start()

    def build(section):
        rows = lax.broadcasted_iota(jnp.int32, (BAND, 2 * BEAMS), 0)
        for child in range(2):
            starts = starts_ref[section, child : child + 1, :]
            shift = jnp.bitwise_and(starts, BAND - 1)
            band = values_ref[section, child].astype(F32)
            for bit in (1, 2, 4, 8):
                rolled = jnp.concatenate([band[BAND - bit :], band[: BAND - bit]], axis=0)
                band = jnp.where(jnp.bitwise_and(shift, bit) != 0, rolled, band)
            home = starts - shift + jnp.where(rows < shift, BAND, 0)
            for first in range(0, BEAMS, BAND):
                matrices[section, child * BEAMS + first : child * BEAMS + first + BAND, :] = (
                    jnp.where(home == first, band, 0.0).astype(BF16)
                )

    def prepare(section, first_bin):
        rate, phase = rates_ref[section] / swath, phases_ref[section]
        offsets = offsets_ref[section]
        upper = (UPPER1, UPPER2)[section - 1]
        starts = [
            unit(phase + rate * ((first_bin + place_of(chunk, upper, me)).astype(F32) + 0.5))
            for chunk in range(2)
        ]
        short, long = unit(rate), unit(rate * 16.0)
        for sub in range(GROUP):
            weights[section, sub] = spread(taps_ref[sub, section], offsets[sub : sub + 1, :])
            near = ladder(nothing, row_of(short, sub))
            for c in range(2):
                for half in range(2):
                    fine[section, sub, c, half * 8 : half * 8 + 8] = near[half][c]
            for chunk in range(2):
                far = ladder(row_of(starts[chunk], sub), row_of(long, sub))[0]
                coarse[section - 1, sub, chunk, 0], coarse[section - 1, sub, chunk, 1] = far

    first_bin = rng * BINS + me * BLOCK
    loads[5].wait()
    loads[6].wait()
    build(0)
    prepare(1, first_bin - 4)
    build(1)
    prepare(2, first_bin)
    build(2)

    @pl.when(jnp.logical_and(even, has_after))
    def _():
        pl.semaphore_wait(credit.at[0], 1)
        edge_copy(0).start()

    @pl.when(jnp.logical_and(even, has_before))
    def _():
        pl.semaphore_wait(credit.at[1], 1)
        edge_copy(1).start()

    for side, there, first in ((0, has_before, 0), (1, has_after, BINS + EDGE)):

        @pl.when(there)
        def _():
            edge_copy(side).wait_recv()
            for part in range(2):
                for half in range(2):
                    raw[part, half, first : first + EDGE, :] = edge_in[
                        side, part, :, half * 128 : half * 128 + 128
                    ].astype(F32)

        @pl.when(jnp.logical_not(there))
        def _():
            raw[:, :, first : first + EDGE, :] = jnp.zeros((2, 2, EDGE, 128), F32)

    for tile in (0, TURNED // 16 - 1):
        turn_own(
            raw.at[:, :, tile * 16 : tile * 16 + 32, :],
            1,
            [coarse0[tile // 8, c] for c in range(2)],
            tile * 16,
        )

    for k in order:

        @pl.when(jnp.logical_not(inner(peers[k])))
        def _():
            in_copy(1, k, peers[k]).start()

    own_in_copy(1).start()

    def merge(section, turned, first, rows):
        left = jnp.concatenate(
            [turned[k, :, :, pl.ds(first, rows), :].reshape(GROUP * rows, BEAMS) for k in range(2)],
            axis=1,
        )
        return jnp.dot(left, matrices[section], preferred_element_type=F32)

    def place(section, group, side):
        low = group % 2 ** section
        return (group - low) * 2 + side * 2 ** section + low

    def keep(section, product, image, first, rows):
        for group in range(4):
            for side in range(2):
                for half in range(2):
                    lanes = slice(side * BEAMS + half * 128, side * BEAMS + half * 128 + 128)
                    image[place(section, group, side), :, half, pl.ds(first, rows), :] = product[
                        group * 2 * rows : (group + 1) * 2 * rows, lanes
                    ].reshape(2, rows, 128)

    def turn(section, chunk, image, turned, first, rows):
        def step(sub, carry):
            child = lax.rem(sub // 2 ** section, 2)
            low = lax.rem(sub, 2 ** section)
            group = sub // 2 ** (section + 1) * 2 ** section + low
            for half in range(2):
                lanes = slice(half * 128, half * 128 + 128)
                taps = [weights[section, sub, j : j + 1, lanes] for j in range(WIDTH)]
                near = [fine[section, sub, c, :, lanes] for c in range(2)]
                source = image.at[sub, :, half, pl.ds(first, rows + 8), :]
                for row in range(0, rows, 16):

                    def load(part, shift):
                        return source[part, row + shift : row + shift + 16, :]

                    tile = row // 16
                    real, imag = turn_tile(
                        load,
                        taps,
                        [
                            coarse[section - 1, sub, chunk, c, tile : tile + 1, lanes]
                            for c in range(2)
                        ],
                        near,
                    )
                    target = pl.ds(pl.multiple_of(first + row, 16), 16)
                    turned[child, group, 0, target, lanes] = real.astype(BF16)
                    turned[child, group, 1, target, lanes] = imag.astype(BF16)
            return carry

        lax.fori_loop(0, GROUP, step, 0)

    def out_rows(chunk):
        return pl.ds(pl.multiple_of(me * BLOCK + place_of(chunk, UPPER2, me), 16), TURN2[chunk])

    def out_copy(chunk, k):
        return pltpu.make_async_remote_copy(
            src_ref=done.at[chunk, peers[k]],
            dst_ref=got.at[:, out_rows(chunk), :],
            send_sem=out_send.at[chunk, k],
            recv_sem=out_recv.at[chunk, k],
            device_id=(base + peers[k], rng),
            device_id_type=MESH,
        )

    def own_out_copy(chunk):
        return pltpu.make_async_copy(
            done.at[chunk, me], got.at[:, out_rows(chunk), :], own_sem.at[2 + chunk]
        )

    low_end = jnp.logical_and(rng == 0, me == 0)
    high_end = jnp.logical_and(rng == ranges - 1, me == GROUP - 1)
    image1[:, :, :, SENT : SENT + 8, :] = jnp.zeros((GROUP, 2, 2, 8, 128), F32)

    for chunk in range(2):
        for k in range(1, GROUP):
            in_copy(chunk, k, me).wait_recv()
        own_in_copy(chunk).wait()
        first, rows = in_rows(chunk, me)
        keep(0, merge(0, got0, first, rows), image1, first, rows)
        if chunk == 1:

            @pl.when(low_end)
            def _():
                image1[:, :, :, 0:8, :] = jnp.zeros((GROUP, 2, 2, 8, 128), F32)

            @pl.when(high_end)
            def _():
                image1[:, :, :, SENT - 8 : SENT, :] = jnp.zeros((GROUP, 2, 2, 8, 128), F32)

        first, rows = place_of(chunk, UPPER1, me), TURN1[chunk]
        turn(1, chunk, image1, turned1, first, rows)
        keep(1, merge(1, turned1, first, rows), image2, first, rows)
        if chunk == 1:

            @pl.when(low_end)
            def _():
                image2[:, :, :, 0:4, :] = jnp.zeros((GROUP, 2, 2, 4, 128), F32)

            @pl.when(high_end)
            def _():
                image2[:, :, :, BLOCK + 4 : BLOCK + 8, :] = jnp.zeros((GROUP, 2, 2, 4, 128), F32)

        first, rows = place_of(chunk, UPPER2, me), TURN2[chunk]
        turn(2, chunk, image2, turned2, first, rows)
        product = merge(2, turned2, first, rows)
        for group in range(4):
            for side in range(2):
                done[chunk, place(2, group, side)] = (
                    product[
                        group * 2 * rows : (group + 1) * 2 * rows,
                        side * BEAMS : (side + 1) * BEAMS,
                    ]
                    .reshape(2, rows, BEAMS)
                    .astype(BF16)
                )
        for k in order:
            out_copy(chunk, k).start()
        own_out_copy(chunk).start()

    for chunk in range(2):
        own_out_copy(chunk).wait()
        for k in range(1, GROUP):
            out_copy(chunk, k).wait_recv()
    for k in range(1, GROUP):
        for chunk in range(2):
            in_copy(chunk, k, peers[k]).wait_send()
            out_copy(chunk, k).wait_send()

    @pl.when(has_after)
    def _():
        edge_copy(0).wait_send()

    @pl.when(has_before)
    def _():
        edge_copy(1).wait_send()


def finish(got_hbm, out_hbm, got, spaced, packed, loaded, sent):
    beams = BEAMS // PIECES
    eye = identity(beams)
    loads, copies = [], []
    for piece in range(PIECES):
        lanes = slice(piece * beams, (piece + 1) * beams)
        loads.append(
            pltpu.make_async_copy(got_hbm.at[:, :, lanes], got.at[piece], loaded.at[piece])
        )
        loads[-1].start()
    for piece in range(PIECES):
        first = piece * beams
        loads[piece].wait()
        for block in range(GROUP):
            for part in range(2):
                spaced[piece, pl.ds(2 * block + part, beams, stride=PITCH), :] = nt_dot(
                    eye, got[piece, part, block * BLOCK : (block + 1) * BLOCK, :]
                )
        for beam in range(beams):
            start = PITCH * beam
            packed[first + beam] = spaced[piece, start : start + 2 * GROUP, :].astype(BF16)
        copies.append(
            pltpu.make_async_copy(
                packed.at[first : first + beams],
                out_hbm.at[first : first + beams],
                sent.at[piece],
            )
        )
        copies[-1].start()
    for copy in copies:
        copy.wait()


def body(subimages, taps, tap_offsets, rates, phases, band_values, band_starts):
    ranges = lax.axis_size("range")
    blocks = subimages.reshape(BEAMS, 2, GROUP, BLOCK).transpose(0, 2, 1, 3)
    blocks = blocks.reshape(BEAMS, 2 * GROUP, BLOCK)
    merged = pl.pallas_call(
        functools.partial(kernel, ranges),
        out_shape=jax.ShapeDtypeStruct((2, BINS, BEAMS), BF16),
        in_specs=[pl.BlockSpec(memory_space=pl.ANY)] * 7,
        out_specs=pl.BlockSpec(memory_space=pl.ANY),
        scratch_shapes=[
            pltpu.VMEM((BEAMS, 2 * GROUP, BLOCK), BF16),
            pltpu.VMEM((GROUP, 3, TAPS, BEAMS), F32),
            pltpu.VMEM((3, GROUP, BEAMS), jnp.int32),
            pltpu.VMEM((3, GROUP, BEAMS), F32),
            pltpu.VMEM((3, GROUP, BEAMS), F32),
            pltpu.VMEM((3, 2, BAND, 2 * BEAMS), BF16),
            pltpu.VMEM((3, 2, 2 * BEAMS), jnp.int32),
            pltpu.VMEM((BEAMS * PITCH, BLOCK), F32),
            pltpu.SemaphoreType.DMA((7,)),
            pltpu.VMEM((2, 2, BINS + 2 * EDGE, 128), F32),
            pltpu.VMEM((2, 2, EDGE, BEAMS), BF16),
            pltpu.VMEM((2, 2, EDGE, BEAMS), BF16),
            pltpu.VMEM((2, TURNED, BEAMS), BF16),
            pltpu.VMEM((2, 4, 2, SENT, BEAMS), BF16),
            pltpu.VMEM((GROUP, 2, 2, SENT + 8, 128), F32),
            pltpu.VMEM((2, 4, 2, SENT, BEAMS), BF16),
            pltpu.VMEM((GROUP, 2, 2, SENT, 128), F32),
            pltpu.VMEM((2, 4, 2, BLOCK, BEAMS), BF16),
            pltpu.VMEM((2, GROUP, 2, BLOCK // 2, BEAMS), BF16),
            pltpu.VMEM((3, 2 * BEAMS, 2 * BEAMS), BF16),
            pltpu.VMEM((3, GROUP, 16, BEAMS), F32),
            pltpu.VMEM((2, GROUP, 2, 2, 8, BEAMS), F32),
            pltpu.VMEM((3, GROUP, 2, 16, BEAMS), F32),
            pltpu.VMEM((GROUP + 1, 2, 8, BEAMS), F32),
            pltpu.SemaphoreType.REGULAR((2,)),
            pltpu.SemaphoreType.DMA((2,)),
            pltpu.SemaphoreType.DMA((2,)),
            pltpu.SemaphoreType.DMA((2, GROUP)),
            pltpu.SemaphoreType.DMA((2, GROUP)),
            pltpu.SemaphoreType.DMA((2, GROUP)),
            pltpu.SemaphoreType.DMA((2, GROUP)),
            pltpu.SemaphoreType.DMA((4,)),
        ],
        compiler_params=pltpu.CompilerParams(
            collective_id=0, has_side_effects=True, vmem_limit_bytes=58 * 2 ** 20
        ),
    )(
        blocks,
        jnp.transpose(taps, (0, 1, 3, 2)),
        jnp.transpose(tap_offsets, (1, 0, 2)),
        jnp.transpose(rates, (1, 0, 2)),
        jnp.transpose(phases, (1, 0, 2)),
        jnp.transpose(band_values, (0, 1, 3, 2)),
        band_starts,
    )
    merged = pl.pallas_call(
        finish,
        out_shape=jax.ShapeDtypeStruct((BEAMS, 2 * GROUP, BLOCK), BF16),
        in_specs=[pl.BlockSpec(memory_space=pl.ANY)],
        out_specs=pl.BlockSpec(memory_space=pl.ANY),
        scratch_shapes=[
            pltpu.VMEM((PIECES, 2, BINS, BEAMS // PIECES), BF16),
            pltpu.VMEM((PIECES, BEAMS // PIECES * PITCH, BLOCK), F32),
            pltpu.VMEM((BEAMS, 2 * GROUP, BLOCK), BF16),
            pltpu.SemaphoreType.DMA((PIECES,)),
            pltpu.SemaphoreType.DMA((PIECES,)),
        ],
        compiler_params=pltpu.CompilerParams(vmem_limit_bytes=58 * 2 ** 20),
    )(merged)
    merged = merged.reshape(BEAMS, GROUP, 2, BLOCK).transpose(0, 2, 1, 3)
    return merged.reshape(1, BEAMS, 2, BINS)


def solution(mesh):
    placed = (P("pulse", None, None, "range"), P(), P(), P(), P(), P(), P())
    return jax.shard_map(
        body, mesh=mesh, in_specs=placed, out_specs=P("pulse", None, None, "range"), check_vma=False
    )
```

```python
import functools

import jax
import jax.numpy as jnp
from jax import lax
from jax.experimental import pallas as pl
from jax.experimental.pallas import tpu as pltpu
from jax.sharding import PartitionSpec as P

MESH = pl.DeviceIdType.MESH
F32 = jnp.float32
BF16 = jnp.bfloat16

BEAMS = 256
BAND = 16
TAPS = 4
WIDTH = 9
GROUP = 8
BINS = 1024
BLOCK = BINS // GROUP
EDGE = 16
PIECES = 2
PITCH = 17
SENT = BLOCK + 16
TURNED = BINS + 16

TURN0, TURN1, TURN2 = (96, 48), (80, 64), (64, 64)
UPPER0, UPPER1, UPPER2 = (48, 96), (64, 80), (64, 64)


def nt_dot(left, right):
    return lax.dot_general(left, right, (((1,), (1,)), ((), ())), preferred_element_type=F32)


def identity(size):
    rows = lax.broadcasted_iota(jnp.int32, (size, size), 0)
    columns = lax.broadcasted_iota(jnp.int32, (size, size), 1)
    return jnp.where(rows == columns, 1.0, 0.0).astype(BF16)


def flip(index, bits):
    return sum(lax.rem(index // bit + bits // bit, 2) * bit for bit in (1, 2, 4))


def spread(taps, offset):
    shifts = lax.broadcasted_iota(jnp.int32, (16, BEAMS), 0) - offset
    weights = jnp.zeros((16, BEAMS), F32)
    for tap in range(TAPS):
        weights = weights + jnp.where(shifts == tap, taps[tap : tap + 1, :], 0.0)
    return weights


def times(a, b):
    return a[0] * b[0] - a[1] * b[1], a[1] * b[0] + a[0] * b[1]


def unit(angle):
    return jnp.cos(angle), jnp.sin(angle)


def ladder(first, step):
    rows = lax.broadcasted_iota(jnp.int32, (8, BEAMS), 0)
    low = first
    for bit in (1, 2, 4):
        taken = jnp.bitwise_and(rows, bit) != 0
        low = times(low, (jnp.where(taken, step[0], 1.0), jnp.where(taken, step[1], 0.0)))
        step = times(step, step)
    return low, times(low, step)


def row_of(pair, row):
    return tuple(jnp.broadcast_to(value[row : row + 1, :], (8, BEAMS)) for value in pair)


def turn_tile(load, weights, coarse, fine):
    real = load(0, 0) * weights[0]
    imag = load(1, 0) * weights[0]
    for shift in range(1, WIDTH):
        real = real + load(0, shift) * weights[shift]
        imag = imag + load(1, shift) * weights[shift]
    cosine = coarse[0] * fine[0] - coarse[1] * fine[1]
    sine = coarse[1] * fine[0] + coarse[0] * fine[1]
    return real * cosine - imag * sine, real * sine + imag * cosine


def kernel(
    ranges,
    x_hbm, taps_hbm, offsets_hbm, rates_hbm, phases_hbm, values_hbm, starts_hbm,
    got,
    x_ref, taps_ref, offsets_ref, rates_ref, phases_ref, values_ref, starts_ref, spaced, load_sem,
    raw, edge_out, edge_in, turned0, got0, image1, turned1, image2, turned2, done,
    matrices, weights, coarse, fine, coarse0,
    credit, edge_send, edge_recv, in_send, in_recv, out_send, out_recv, own_sem,
):
    pulse = lax.axis_index("pulse")
    rng = lax.axis_index("range")
    me = lax.rem(pulse, GROUP)
    base = pulse - me
    swath = float(BINS * ranges)
    after, before = lax.rem(rng + 1, ranges), lax.rem(rng + ranges - 1, ranges)
    peers = [flip(me, k) for k in range(GROUP)]

    even = lax.rem(rng, 2) == 0
    has_before, has_after = rng > 0, rng < ranges - 1

    def place_of(chunk, upper, device):
        flipped = 1 - jnp.minimum(device, 1)
        return pl.multiple_of(upper[chunk] * (flipped if chunk == 0 else 1 - flipped), 16)

    rows8 = pl.ds(pl.multiple_of(base, GROUP), GROUP)
    pieces = [slice(i * BEAMS // 4, (i + 1) * BEAMS // 4) for i in range(4)]
    pairs = [(x_hbm.at[piece], x_ref.at[piece]) for piece in pieces] + [
        (rates_hbm.at[:, rows8, :], rates_ref),
        (phases_hbm.at[:, rows8, :], phases_ref),
        (offsets_hbm.at[:, rows8, :], offsets_ref),
        (taps_hbm.at[rows8], taps_ref),
        (values_hbm, values_ref),
        (starts_hbm, starts_ref),
    ]
    loads = [
        pltpu.make_async_copy(source, kept, load_sem.at[i])
        for i, (source, kept) in enumerate(pairs)
    ]
    for load in loads:
        load.start()

    barrier = pltpu.get_barrier_semaphore()
    for k in range(1, GROUP):
        pl.semaphore_signal(barrier, 1, device_id=(base + peers[k], rng), device_id_type=MESH)

    @pl.when(jnp.logical_and(even, has_after))
    def _():
        pl.semaphore_signal(barrier, 1, device_id=(pulse, after), device_id_type=MESH)

    @pl.when(jnp.logical_and(even, has_before))
    def _():
        pl.semaphore_signal(barrier, 1, device_id=(pulse, before), device_id_type=MESH)

    for load in loads[4:8]:
        load.wait()

    mine = lax.broadcasted_iota(jnp.int32, (8, BEAMS), 0) == me

    def own(ref):
        value = jnp.sum(jnp.where(mine, ref[0], 0), axis=0, keepdims=True)
        return jnp.broadcast_to(value, (8, BEAMS))

    weights[0, 0] = spread(taps_ref[me, 0], own(offsets_ref)[0:1, :])
    rate, phase = own(rates_ref) / swath, own(phases_ref)
    nothing = jnp.ones_like(rate), jnp.zeros_like(rate)
    close = ladder(nothing, unit(rate))
    tiles = ladder(unit(phase + rate * ((rng * BINS - 8).astype(F32) + 0.5)), unit(rate * 16.0))
    blocks = ladder(nothing, unit(rate * 128.0))
    for block in range(GROUP + 1):
        far = times(tiles[0], row_of(blocks[block // 8], block % 8))
        coarse0[block, 0], coarse0[block, 1] = far
    for c in range(2):
        fine[0, 0, c, 0:8], fine[0, 0, c, 8:16] = close[0][c], close[1][c]

    eye = identity(BLOCK)
    for load, piece in zip(loads[:4], pieces):
        load.wait()
        for beam in range(piece.start, piece.stop):
            spaced[PITCH * beam : PITCH * beam + 2 * GROUP, :] = x_ref[beam].astype(F32)
    for block in range(GROUP):
        for part in range(2):
            picked = spaced[pl.ds(2 * block + part, BEAMS, stride=PITCH), :]
            rows = nt_dot(eye, picked.astype(BF16))
            for half in range(2):
                raw[part, half, EDGE + block * BLOCK : EDGE + (block + 1) * BLOCK, :] = rows[
                    :, half * 128 : half * 128 + 128
                ]
    for part in range(2):
        for half in range(2):
            lanes = slice(half * 128, half * 128 + 128)
            edge_out[0, part, :, lanes] = raw[part, half, BINS : BINS + EDGE, :].astype(BF16)
            edge_out[1, part, :, lanes] = raw[part, half, EDGE : 2 * EDGE, :].astype(BF16)

    def edge_copy(side):
        return pltpu.make_async_remote_copy(
            src_ref=edge_out.at[side],
            dst_ref=edge_in.at[side],
            send_sem=edge_send.at[side],
            recv_sem=edge_recv.at[side],
            device_id=(pulse, after if side == 0 else before),
            device_id_type=MESH,
        )

    @pl.when(even)
    def _():
        pl.semaphore_wait(barrier, GROUP - 1)

    @pl.when(jnp.logical_not(even))
    def _():
        pl.semaphore_wait(barrier, GROUP + jnp.where(has_after, 1, 0))
        pl.semaphore_signal(
            credit.at[0], 1, device_id=(pulse, before), device_id_type=MESH
        )
        edge_copy(1).start()

        @pl.when(has_after)
        def _():
            pl.semaphore_signal(
                credit.at[1], 1, device_id=(pulse, after), device_id_type=MESH
            )
            edge_copy(0).start()

    def turn_own(near, tiles, far, first):
        for half in range(2):
            lanes = slice(half * 128, half * 128 + 128)
            taps = [weights[0, 0, j : j + 1, lanes] for j in range(WIDTH)]
            close = [fine[0, 0, c, :, lanes] for c in range(2)]
            for tile in range(tiles):

                def load(part, shift):
                    return near[part, half, 16 * tile + 4 + shift : 16 * tile + 20 + shift, :]

                real, imag = turn_tile(
                    load, taps, [far[c][tile : tile + 1, lanes] for c in range(2)], close
                )
                rows = pl.ds(pl.multiple_of(first + 16 * tile, 16), 16)
                turned0[0, rows, lanes] = real.astype(BF16)
                turned0[1, rows, lanes] = imag.astype(BF16)

    def in_rows(chunk, device):
        return place_of(chunk, UPPER0, device), TURN0[chunk]

    def in_copy(chunk, k, peer):
        first, rows = in_rows(chunk, peer)
        return pltpu.make_async_remote_copy(
            src_ref=turned0.at[:, pl.ds(pl.multiple_of(peer * BLOCK + first, 16), rows), :],
            dst_ref=got0.at[lax.rem(me, 2), me // 2, :, pl.ds(first, rows), :],
            send_sem=in_send.at[chunk, k],
            recv_sem=in_recv.at[chunk, k],
            device_id=(base + peer, rng),
            device_id_type=MESH,
        )

    def own_in_copy(chunk):
        first, rows = in_rows(chunk, me)
        return pltpu.make_async_copy(
            turned0.at[:, pl.ds(pl.multiple_of(me * BLOCK + first, 16), rows), :],
            got0.at[lax.rem(me, 2), me // 2, :, pl.ds(first, rows), :],
            own_sem.at[chunk],
        )

    def turn_block(block):
        first = pl.multiple_of(block * BLOCK, BLOCK)
        turn_own(
            raw.at[:, :, pl.ds(first, BLOCK + 16), :],
            BLOCK // 16,
            [coarse0[block, c] for c in range(2)],
            first,
        )

    order = (5, 4, 3, 2, 7, 6, 1)

    def turn_and_send(i, carry):
        k = GROUP - 1 - i
        peer = flip(me, k)
        turn_block(peer)

        @pl.when(jnp.logical_and(peer != 0, k != 0))
        def _():
            in_copy(0, k, peer).start()

        return carry

    lax.fori_loop(0, GROUP, turn_and_send, 0)

    @pl.when(me != 0)
    def _():
        in_copy(0, me, 0).start()

    own_in_copy(0).start()

    def inner(peer):
        return jnp.logical_and(peer > 0, peer < GROUP - 1)

    for k in order:

        @pl.when(inner(peers[k]))
        def _():
            in_copy(1, k, peers[k]).start()

    def build(section):
        rows = lax.broadcasted_iota(jnp.int32, (BAND, 2 * BEAMS), 0)
        for child in range(2):
            starts = starts_ref[section, child : child + 1, :]
            shift = jnp.bitwise_and(starts, BAND - 1)
            band = values_ref[section, child].astype(F32)
            for bit in (1, 2, 4, 8):
                rolled = jnp.concatenate([band[BAND - bit :], band[: BAND - bit]], axis=0)
                band = jnp.where(jnp.bitwise_and(shift, bit) != 0, rolled, band)
            home = starts - shift + jnp.where(rows < shift, BAND, 0)
            for first in range(0, BEAMS, BAND):
                matrices[section, child * BEAMS + first : child * BEAMS + first + BAND, :] = (
                    jnp.where(home == first, band, 0.0).astype(BF16)
                )

    def prepare(section, first_bin):
        rate, phase = rates_ref[section] / swath, phases_ref[section]
        offsets = offsets_ref[section]
        upper = (UPPER1, UPPER2)[section - 1]
        starts = [
            unit(phase + rate * ((first_bin + place_of(chunk, upper, me)).astype(F32) + 0.5))
            for chunk in range(2)
        ]
        short, long = unit(rate), unit(rate * 16.0)
        for sub in range(GROUP):
            weights[section, sub] = spread(taps_ref[sub, section], offsets[sub : sub + 1, :])
            near = ladder(nothing, row_of(short, sub))
            for c in range(2):
                for half in range(2):
                    fine[section, sub, c, half * 8 : half * 8 + 8] = near[half][c]
            for chunk in range(2):
                far = ladder(row_of(starts[chunk], sub), row_of(long, sub))[0]
                coarse[section - 1, sub, chunk, 0], coarse[section - 1, sub, chunk, 1] = far

    first_bin = rng * BINS + me * BLOCK
    loads[8].wait()
    loads[9].wait()
    build(0)
    prepare(1, first_bin - 4)
    build(1)
    prepare(2, first_bin)
    build(2)

    @pl.when(jnp.logical_and(even, has_after))
    def _():
        pl.semaphore_wait(credit.at[0], 1)
        edge_copy(0).start()

    @pl.when(jnp.logical_and(even, has_before))
    def _():
        pl.semaphore_wait(credit.at[1], 1)
        edge_copy(1).start()

    for side, there, first in ((0, has_before, 0), (1, has_after, BINS + EDGE)):

        @pl.when(there)
        def _():
            edge_copy(side).wait_recv()
            for part in range(2):
                for half in range(2):
                    raw[part, half, first : first + EDGE, :] = edge_in[
                        side, part, :, half * 128 : half * 128 + 128
                    ].astype(F32)

        @pl.when(jnp.logical_not(there))
        def _():
            raw[:, :, first : first + EDGE, :] = jnp.zeros((2, 2, EDGE, 128), F32)

    for tile in (0, TURNED // 16 - 1):
        turn_own(
            raw.at[:, :, tile * 16 : tile * 16 + 32, :],
            1,
            [coarse0[tile // 8, c] for c in range(2)],
            tile * 16,
        )

    for k in order:

        @pl.when(jnp.logical_not(inner(peers[k])))
        def _():
            in_copy(1, k, peers[k]).start()

    own_in_copy(1).start()

    def merge(section, turned, first, rows):
        left = jnp.concatenate(
            [turned[k, :, :, pl.ds(first, rows), :].reshape(GROUP * rows, BEAMS) for k in range(2)],
            axis=1,
        )
        return jnp.dot(left, matrices[section], preferred_element_type=F32)

    def place(section, group, side):
        low = group % 2 ** section
        return (group - low) * 2 + side * 2 ** section + low

    def keep(section, product, image, first, rows):
        for group in range(4):
            for side in range(2):
                for half in range(2):
                    lanes = slice(side * BEAMS + half * 128, side * BEAMS + half * 128 + 128)
                    image[place(section, group, side), :, half, pl.ds(first, rows), :] = product[
                        group * 2 * rows : (group + 1) * 2 * rows, lanes
                    ].reshape(2, rows, 128)

    def turn(section, chunk, image, turned, first, rows):
        def step(sub, carry):
            child = lax.rem(sub // 2 ** section, 2)
            low = lax.rem(sub, 2 ** section)
            group = sub // 2 ** (section + 1) * 2 ** section + low
            for half in range(2):
                lanes = slice(half * 128, half * 128 + 128)
                taps = [weights[section, sub, j : j + 1, lanes] for j in range(WIDTH)]
                near = [fine[section, sub, c, :, lanes] for c in range(2)]
                source = image.at[sub, :, half, pl.ds(first, rows + 8), :]
                for row in range(0, rows, 16):

                    def load(part, shift):
                        return source[part, row + shift : row + shift + 16, :]

                    tile = row // 16
                    real, imag = turn_tile(
                        load,
                        taps,
                        [
                            coarse[section - 1, sub, chunk, c, tile : tile + 1, lanes]
                            for c in range(2)
                        ],
                        near,
                    )
                    target = pl.ds(pl.multiple_of(first + row, 16), 16)
                    turned[child, group, 0, target, lanes] = real.astype(BF16)
                    turned[child, group, 1, target, lanes] = imag.astype(BF16)
            return carry

        lax.fori_loop(0, GROUP, step, 0)

    def out_rows(chunk):
        return pl.ds(pl.multiple_of(me * BLOCK + place_of(chunk, UPPER2, me), 16), TURN2[chunk])

    def out_copy(chunk, k):
        return pltpu.make_async_remote_copy(
            src_ref=done.at[chunk, peers[k]],
            dst_ref=got.at[:, out_rows(chunk), :],
            send_sem=out_send.at[chunk, k],
            recv_sem=out_recv.at[chunk, k],
            device_id=(base + peers[k], rng),
            device_id_type=MESH,
        )

    def own_out_copy(chunk):
        return pltpu.make_async_copy(
            done.at[chunk, me], got.at[:, out_rows(chunk), :], own_sem.at[2 + chunk]
        )

    low_end = jnp.logical_and(rng == 0, me == 0)
    high_end = jnp.logical_and(rng == ranges - 1, me == GROUP - 1)
    image1[:, :, :, SENT : SENT + 8, :] = jnp.zeros((GROUP, 2, 2, 8, 128), F32)

    for chunk in range(2):
        for k in range(1, GROUP):
            in_copy(chunk, k, me).wait_recv()
        own_in_copy(chunk).wait()
        first, rows = in_rows(chunk, me)
        keep(0, merge(0, got0, first, rows), image1, first, rows)
        if chunk == 1:

            @pl.when(low_end)
            def _():
                image1[:, :, :, 0:8, :] = jnp.zeros((GROUP, 2, 2, 8, 128), F32)

            @pl.when(high_end)
            def _():
                image1[:, :, :, SENT - 8 : SENT, :] = jnp.zeros((GROUP, 2, 2, 8, 128), F32)

        first, rows = place_of(chunk, UPPER1, me), TURN1[chunk]
        turn(1, chunk, image1, turned1, first, rows)
        keep(1, merge(1, turned1, first, rows), image2, first, rows)
        if chunk == 1:

            @pl.when(low_end)
            def _():
                image2[:, :, :, 0:4, :] = jnp.zeros((GROUP, 2, 2, 4, 128), F32)

            @pl.when(high_end)
            def _():
                image2[:, :, :, BLOCK + 4 : BLOCK + 8, :] = jnp.zeros((GROUP, 2, 2, 4, 128), F32)

        first, rows = place_of(chunk, UPPER2, me), TURN2[chunk]
        turn(2, chunk, image2, turned2, first, rows)
        product = merge(2, turned2, first, rows)
        for group in range(4):
            for side in range(2):
                done[chunk, place(2, group, side)] = (
                    product[
                        group * 2 * rows : (group + 1) * 2 * rows,
                        side * BEAMS : (side + 1) * BEAMS,
                    ]
                    .reshape(2, rows, BEAMS)
                    .astype(BF16)
                )
        for k in order:
            out_copy(chunk, k).start()
        own_out_copy(chunk).start()

    for chunk in range(2):
        own_out_copy(chunk).wait()
        for k in range(1, GROUP):
            out_copy(chunk, k).wait_recv()
    for k in range(1, GROUP):
        for chunk in range(2):
            in_copy(chunk, k, peers[k]).wait_send()
            out_copy(chunk, k).wait_send()

    @pl.when(has_after)
    def _():
        edge_copy(0).wait_send()

    @pl.when(has_before)
    def _():
        edge_copy(1).wait_send()


def finish(got_hbm, out_hbm, got, spaced, packed, loaded, sent):
    beams = BEAMS // PIECES
    eye = identity(beams)
    loads, copies = [], []
    for piece in range(PIECES):
        lanes = slice(piece * beams, (piece + 1) * beams)
        loads.append(
            pltpu.make_async_copy(got_hbm.at[:, :, lanes], got.at[piece], loaded.at[piece])
        )
        loads[-1].start()
    for piece in range(PIECES):
        first = piece * beams
        loads[piece].wait()
        for block in range(GROUP):
            for part in range(2):
                spaced[piece, pl.ds(2 * block + part, beams, stride=PITCH), :] = jnp.transpose(
                    got[piece, part, block * BLOCK : (block + 1) * BLOCK, :].astype(F32)
                )
        for beam in range(beams):
            start = PITCH * beam
            packed[first + beam] = spaced[piece, start : start + 2 * GROUP, :].astype(BF16)
        copies.append(
            pltpu.make_async_copy(
                packed.at[first : first + beams],
                out_hbm.at[first : first + beams],
                sent.at[piece],
            )
        )
        copies[-1].start()
    for copy in copies:
        copy.wait()


def body(subimages, taps, tap_offsets, rates, phases, band_values, band_starts):
    ranges = lax.axis_size("range")
    blocks = subimages.reshape(BEAMS, 2, GROUP, BLOCK).transpose(0, 2, 1, 3)
    blocks = blocks.reshape(BEAMS, 2 * GROUP, BLOCK)
    merged = pl.pallas_call(
        functools.partial(kernel, ranges),
        out_shape=jax.ShapeDtypeStruct((2, BINS, BEAMS), BF16),
        in_specs=[pl.BlockSpec(memory_space=pl.ANY)] * 7,
        out_specs=pl.BlockSpec(memory_space=pl.ANY),
        scratch_shapes=[
            pltpu.VMEM((BEAMS, 2 * GROUP, BLOCK), BF16),
            pltpu.VMEM((GROUP, 3, TAPS, BEAMS), F32),
            pltpu.VMEM((3, GROUP, BEAMS), jnp.int32),
            pltpu.VMEM((3, GROUP, BEAMS), F32),
            pltpu.VMEM((3, GROUP, BEAMS), F32),
            pltpu.VMEM((3, 2, BAND, 2 * BEAMS), BF16),
            pltpu.VMEM((3, 2, 2 * BEAMS), jnp.int32),
            pltpu.VMEM((BEAMS * PITCH, BLOCK), F32),
            pltpu.SemaphoreType.DMA((10,)),
            pltpu.VMEM((2, 2, BINS + 2 * EDGE, 128), F32),
            pltpu.VMEM((2, 2, EDGE, BEAMS), BF16),
            pltpu.VMEM((2, 2, EDGE, BEAMS), BF16),
            pltpu.VMEM((2, TURNED, BEAMS), BF16),
            pltpu.VMEM((2, 4, 2, SENT, BEAMS), BF16),
            pltpu.VMEM((GROUP, 2, 2, SENT + 8, 128), F32),
            pltpu.VMEM((2, 4, 2, SENT, BEAMS), BF16),
            pltpu.VMEM((GROUP, 2, 2, SENT, 128), F32),
            pltpu.VMEM((2, 4, 2, BLOCK, BEAMS), BF16),
            pltpu.VMEM((2, GROUP, 2, BLOCK // 2, BEAMS), BF16),
            pltpu.VMEM((3, 2 * BEAMS, 2 * BEAMS), BF16),
            pltpu.VMEM((3, GROUP, 16, BEAMS), F32),
            pltpu.VMEM((2, GROUP, 2, 2, 8, BEAMS), F32),
            pltpu.VMEM((3, GROUP, 2, 16, BEAMS), F32),
            pltpu.VMEM((GROUP + 1, 2, 8, BEAMS), F32),
            pltpu.SemaphoreType.REGULAR((2,)),
            pltpu.SemaphoreType.DMA((2,)),
            pltpu.SemaphoreType.DMA((2,)),
            pltpu.SemaphoreType.DMA((2, GROUP)),
            pltpu.SemaphoreType.DMA((2, GROUP)),
            pltpu.SemaphoreType.DMA((2, GROUP)),
            pltpu.SemaphoreType.DMA((2, GROUP)),
            pltpu.SemaphoreType.DMA((4,)),
        ],
        compiler_params=pltpu.CompilerParams(
            collective_id=0, has_side_effects=True, vmem_limit_bytes=58 * 2 ** 20
        ),
    )(
        blocks,
        jnp.transpose(taps, (0, 1, 3, 2)),
        jnp.transpose(tap_offsets, (1, 0, 2)),
        jnp.transpose(rates, (1, 0, 2)),
        jnp.transpose(phases, (1, 0, 2)),
        jnp.transpose(band_values, (0, 1, 3, 2)),
        band_starts,
    )
    merged = pl.pallas_call(
        finish,
        out_shape=jax.ShapeDtypeStruct((BEAMS, 2 * GROUP, BLOCK), BF16),
        in_specs=[pl.BlockSpec(memory_space=pl.ANY)],
        out_specs=pl.BlockSpec(memory_space=pl.ANY),
        scratch_shapes=[
            pltpu.VMEM((PIECES, 2, BINS, BEAMS // PIECES), BF16),
            pltpu.VMEM((PIECES, BEAMS // PIECES * PITCH, BLOCK), F32),
            pltpu.VMEM((BEAMS, 2 * GROUP, BLOCK), BF16),
            pltpu.SemaphoreType.DMA((PIECES,)),
            pltpu.SemaphoreType.DMA((PIECES,)),
        ],
        compiler_params=pltpu.CompilerParams(vmem_limit_bytes=58 * 2 ** 20),
    )(merged)
    merged = merged.reshape(BEAMS, GROUP, 2, BLOCK).transpose(0, 2, 1, 3)
    return merged.reshape(1, BEAMS, 2, BINS)


def solution(mesh):
    placed = (P("pulse", None, None, "range"), P(), P(), P(), P(), P(), P())
    return jax.shard_map(
        body, mesh=mesh, in_specs=placed, out_specs=P("pulse", None, None, "range"), check_vma=False
    )
```

```python
import functools

import jax
import jax.numpy as jnp
from jax import lax
from jax.experimental import pallas as pl
from jax.experimental.pallas import tpu as pltpu
from jax.sharding import PartitionSpec as P

MESH = pl.DeviceIdType.MESH
F32 = jnp.float32
BF16 = jnp.bfloat16

BEAMS = 256
BAND = 16
TAPS = 4
WIDTH = 9
GROUP = 8
BINS = 1024
BLOCK = BINS // GROUP
EDGE = 16
PIECES = 2
PITCH = 17
SENT = BLOCK + 16
TURNED = BINS + 16

TURN0, TURN1, TURN2 = (96, 48), (80, 64), (64, 64)
UPPER0, UPPER1, UPPER2 = (48, 96), (64, 80), (64, 64)


def flip(index, bits):
    return sum(lax.rem(index // bit + bits // bit, 2) * bit for bit in (1, 2, 4))


def spread(taps, offset):
    shifts = lax.broadcasted_iota(jnp.int32, (16, BEAMS), 0) - offset
    weights = jnp.zeros((16, BEAMS), F32)
    for tap in range(TAPS):
        weights = weights + jnp.where(shifts == tap, taps[tap : tap + 1, :], 0.0)
    return weights


def times(a, b):
    return a[0] * b[0] - a[1] * b[1], a[1] * b[0] + a[0] * b[1]


def unit(angle):
    return jnp.cos(angle), jnp.sin(angle)


def ladder(first, step):
    rows = lax.broadcasted_iota(jnp.int32, (8, BEAMS), 0)
    low = first
    for bit in (1, 2, 4):
        taken = jnp.bitwise_and(rows, bit) != 0
        low = times(low, (jnp.where(taken, step[0], 1.0), jnp.where(taken, step[1], 0.0)))
        step = times(step, step)
    return low, times(low, step)


def row_of(pair, row):
    return tuple(jnp.broadcast_to(value[row : row + 1, :], (8, BEAMS)) for value in pair)


def turn_tile(load, weights, coarse, fine):
    real = load(0, 0) * weights[0]
    imag = load(1, 0) * weights[0]
    for shift in range(1, WIDTH):
        real = real + load(0, shift) * weights[shift]
        imag = imag + load(1, shift) * weights[shift]
    cosine = coarse[0] * fine[0] - coarse[1] * fine[1]
    sine = coarse[1] * fine[0] + coarse[0] * fine[1]
    return real * cosine - imag * sine, real * sine + imag * cosine


def kernel(
    ranges,
    x_hbm, taps_hbm, offsets_hbm, rates_hbm, phases_hbm, values_hbm, starts_hbm,
    got,
    x_ref, taps_ref, offsets_ref, rates_ref, phases_ref, values_ref, starts_ref, spaced, load_sem,
    raw, edge_out, edge_in, turned0, got0, image1, turned1, image2, turned2, done,
    matrices, weights, coarse, fine, coarse0,
    credit, edge_send, edge_recv, in_send, in_recv, out_send, out_recv, own_sem,
):
    pulse = lax.axis_index("pulse")
    rng = lax.axis_index("range")
    me = lax.rem(pulse, GROUP)
    base = pulse - me
    swath = float(BINS * ranges)
    after, before = lax.rem(rng + 1, ranges), lax.rem(rng + ranges - 1, ranges)
    peers = [flip(me, k) for k in range(GROUP)]

    even = lax.rem(rng, 2) == 0
    has_before, has_after = rng > 0, rng < ranges - 1

    def place_of(chunk, upper, device):
        flipped = 1 - jnp.minimum(device, 1)
        return pl.multiple_of(upper[chunk] * (flipped if chunk == 0 else 1 - flipped), 16)

    rows8 = pl.ds(pl.multiple_of(base, GROUP), GROUP)
    pieces = [slice(i * BEAMS // 4, (i + 1) * BEAMS // 4) for i in range(4)]
    pairs = [(x_hbm.at[piece], x_ref.at[piece]) for piece in pieces] + [
        (rates_hbm.at[:, rows8, :], rates_ref),
        (phases_hbm.at[:, rows8, :], phases_ref),
        (offsets_hbm.at[:, rows8, :], offsets_ref),
        (taps_hbm.at[rows8], taps_ref),
        (values_hbm, values_ref),
        (starts_hbm, starts_ref),
    ]
    loads = [
        pltpu.make_async_copy(source, kept, load_sem.at[i])
        for i, (source, kept) in enumerate(pairs)
    ]
    for load in loads:
        load.start()

    barrier = pltpu.get_barrier_semaphore()
    for k in range(1, GROUP):
        pl.semaphore_signal(barrier, 1, device_id=(base + peers[k], rng), device_id_type=MESH)

    @pl.when(jnp.logical_and(even, has_after))
    def _():
        pl.semaphore_signal(barrier, 1, device_id=(pulse, after), device_id_type=MESH)

    @pl.when(jnp.logical_and(even, has_before))
    def _():
        pl.semaphore_signal(barrier, 1, device_id=(pulse, before), device_id_type=MESH)

    for load in loads[4:8]:
        load.wait()

    mine = lax.broadcasted_iota(jnp.int32, (8, BEAMS), 0) == me

    def own(ref):
        value = jnp.sum(jnp.where(mine, ref[0], 0), axis=0, keepdims=True)
        return jnp.broadcast_to(value, (8, BEAMS))

    weights[0, 0] = spread(taps_ref[me, 0], own(offsets_ref)[0:1, :])
    rate, phase = own(rates_ref) / swath, own(phases_ref)
    nothing = jnp.ones_like(rate), jnp.zeros_like(rate)
    close = ladder(nothing, unit(rate))
    tiles = ladder(unit(phase + rate * ((rng * BINS - 8).astype(F32) + 0.5)), unit(rate * 16.0))
    blocks = ladder(nothing, unit(rate * 128.0))
    for block in range(GROUP + 1):
        far = times(tiles[0], row_of(blocks[block // 8], block % 8))
        coarse0[block, 0], coarse0[block, 1] = far
    for c in range(2):
        fine[0, 0, c, 0:8], fine[0, 0, c, 8:16] = close[0][c], close[1][c]

    for load, piece in zip(loads[:4], pieces):
        load.wait()
        for beam in range(piece.start, piece.stop):
            spaced[PITCH * beam : PITCH * beam + 2 * GROUP, :] = x_ref[beam].astype(F32)
    for block in range(GROUP):
        for part in range(2):
            picked = spaced[pl.ds(2 * block + part, BEAMS, stride=PITCH), :]
            rows = jnp.transpose(picked)
            for half in range(2):
                raw[part, half, EDGE + block * BLOCK : EDGE + (block + 1) * BLOCK, :] = rows[
                    :, half * 128 : half * 128 + 128
                ]
    for part in range(2):
        for half in range(2):
            lanes = slice(half * 128, half * 128 + 128)
            edge_out[0, part, :, lanes] = raw[part, half, BINS : BINS + EDGE, :].astype(BF16)
            edge_out[1, part, :, lanes] = raw[part, half, EDGE : 2 * EDGE, :].astype(BF16)

    def edge_copy(side):
        return pltpu.make_async_remote_copy(
            src_ref=edge_out.at[side],
            dst_ref=edge_in.at[side],
            send_sem=edge_send.at[side],
            recv_sem=edge_recv.at[side],
            device_id=(pulse, after if side == 0 else before),
            device_id_type=MESH,
        )

    @pl.when(even)
    def _():
        pl.semaphore_wait(barrier, GROUP - 1)

    @pl.when(jnp.logical_not(even))
    def _():
        pl.semaphore_wait(barrier, GROUP + jnp.where(has_after, 1, 0))
        pl.semaphore_signal(
            credit.at[0], 1, device_id=(pulse, before), device_id_type=MESH
        )
        edge_copy(1).start()

        @pl.when(has_after)
        def _():
            pl.semaphore_signal(
                credit.at[1], 1, device_id=(pulse, after), device_id_type=MESH
            )
            edge_copy(0).start()

    def turn_own(near, tiles, far, first):
        for half in range(2):
            lanes = slice(half * 128, half * 128 + 128)
            taps = [weights[0, 0, j : j + 1, lanes] for j in range(WIDTH)]
            close = [fine[0, 0, c, :, lanes] for c in range(2)]
            for tile in range(tiles):

                def load(part, shift):
                    return near[part, half, 16 * tile + 4 + shift : 16 * tile + 20 + shift, :]

                real, imag = turn_tile(
                    load, taps, [far[c][tile : tile + 1, lanes] for c in range(2)], close
                )
                rows = pl.ds(pl.multiple_of(first + 16 * tile, 16), 16)
                turned0[0, rows, lanes] = real.astype(BF16)
                turned0[1, rows, lanes] = imag.astype(BF16)

    def in_rows(chunk, device):
        return place_of(chunk, UPPER0, device), TURN0[chunk]

    def in_copy(chunk, k, peer):
        first, rows = in_rows(chunk, peer)
        return pltpu.make_async_remote_copy(
            src_ref=turned0.at[:, pl.ds(pl.multiple_of(peer * BLOCK + first, 16), rows), :],
            dst_ref=got0.at[lax.rem(me, 2), me // 2, :, pl.ds(first, rows), :],
            send_sem=in_send.at[chunk, k],
            recv_sem=in_recv.at[chunk, k],
            device_id=(base + peer, rng),
            device_id_type=MESH,
        )

    def own_in_copy(chunk):
        first, rows = in_rows(chunk, me)
        return pltpu.make_async_copy(
            turned0.at[:, pl.ds(pl.multiple_of(me * BLOCK + first, 16), rows), :],
            got0.at[lax.rem(me, 2), me // 2, :, pl.ds(first, rows), :],
            own_sem.at[chunk],
        )

    def turn_block(block):
        first = pl.multiple_of(block * BLOCK, BLOCK)
        turn_own(
            raw.at[:, :, pl.ds(first, BLOCK + 16), :],
            BLOCK // 16,
            [coarse0[block, c] for c in range(2)],
            first,
        )

    order = (5, 4, 3, 2, 7, 6, 1)

    def turn_and_send(i, carry):
        k = GROUP - 1 - i
        peer = flip(me, k)
        turn_block(peer)

        @pl.when(jnp.logical_and(peer != 0, k != 0))
        def _():
            in_copy(0, k, peer).start()

        return carry

    lax.fori_loop(0, GROUP, turn_and_send, 0)

    @pl.when(me != 0)
    def _():
        in_copy(0, me, 0).start()

    own_in_copy(0).start()

    def inner(peer):
        return jnp.logical_and(peer > 0, peer < GROUP - 1)

    for k in order:

        @pl.when(inner(peers[k]))
        def _():
            in_copy(1, k, peers[k]).start()

    def build(section):
        rows = lax.broadcasted_iota(jnp.int32, (BAND, 2 * BEAMS), 0)
        for child in range(2):
            starts = starts_ref[section, child : child + 1, :]
            shift = jnp.bitwise_and(starts, BAND - 1)
            band = values_ref[section, child].astype(F32)
            for bit in (1, 2, 4, 8):
                rolled = jnp.concatenate([band[BAND - bit :], band[: BAND - bit]], axis=0)
                band = jnp.where(jnp.bitwise_and(shift, bit) != 0, rolled, band)
            home = starts - shift + jnp.where(rows < shift, BAND, 0)
            for first in range(0, BEAMS, BAND):
                matrices[section, child * BEAMS + first : child * BEAMS + first + BAND, :] = (
                    jnp.where(home == first, band, 0.0).astype(BF16)
                )

    def prepare(section, first_bin):
        rate, phase = rates_ref[section] / swath, phases_ref[section]
        offsets = offsets_ref[section]
        upper = (UPPER1, UPPER2)[section - 1]
        starts = [
            unit(phase + rate * ((first_bin + place_of(chunk, upper, me)).astype(F32) + 0.5))
            for chunk in range(2)
        ]
        short, long = unit(rate), unit(rate * 16.0)
        for sub in range(GROUP):
            weights[section, sub] = spread(taps_ref[sub, section], offsets[sub : sub + 1, :])
            near = ladder(nothing, row_of(short, sub))
            for c in range(2):
                for half in range(2):
                    fine[section, sub, c, half * 8 : half * 8 + 8] = near[half][c]
            for chunk in range(2):
                far = ladder(row_of(starts[chunk], sub), row_of(long, sub))[0]
                coarse[section - 1, sub, chunk, 0], coarse[section - 1, sub, chunk, 1] = far

    first_bin = rng * BINS + me * BLOCK
    loads[8].wait()
    loads[9].wait()
    build(0)
    prepare(1, first_bin - 4)
    build(1)
    prepare(2, first_bin)
    build(2)

    @pl.when(jnp.logical_and(even, has_after))
    def _():
        pl.semaphore_wait(credit.at[0], 1)
        edge_copy(0).start()

    @pl.when(jnp.logical_and(even, has_before))
    def _():
        pl.semaphore_wait(credit.at[1], 1)
        edge_copy(1).start()

    for side, there, first in ((0, has_before, 0), (1, has_after, BINS + EDGE)):

        @pl.when(there)
        def _():
            edge_copy(side).wait_recv()
            for part in range(2):
                for half in range(2):
                    raw[part, half, first : first + EDGE, :] = edge_in[
                        side, part, :, half * 128 : half * 128 + 128
                    ].astype(F32)

        @pl.when(jnp.logical_not(there))
        def _():
            raw[:, :, first : first + EDGE, :] = jnp.zeros((2, 2, EDGE, 128), F32)

    for tile in (0, TURNED // 16 - 1):
        turn_own(
            raw.at[:, :, tile * 16 : tile * 16 + 32, :],
            1,
            [coarse0[tile // 8, c] for c in range(2)],
            tile * 16,
        )

    for k in order:

        @pl.when(jnp.logical_not(inner(peers[k])))
        def _():
            in_copy(1, k, peers[k]).start()

    own_in_copy(1).start()

    def merge(section, turned, first, rows):
        left = jnp.concatenate(
            [turned[k, :, :, pl.ds(first, rows), :].reshape(GROUP * rows, BEAMS) for k in range(2)],
            axis=1,
        )
        return jnp.dot(left, matrices[section], preferred_element_type=F32)

    def place(section, group, side):
        low = group % 2 ** section
        return (group - low) * 2 + side * 2 ** section + low

    def keep(section, product, image, first, rows):
        for group in range(4):
            for side in range(2):
                for half in range(2):
                    lanes = slice(side * BEAMS + half * 128, side * BEAMS + half * 128 + 128)
                    image[place(section, group, side), :, half, pl.ds(first, rows), :] = product[
                        group * 2 * rows : (group + 1) * 2 * rows, lanes
                    ].reshape(2, rows, 128)

    def turn(section, chunk, image, turned, first, rows):
        def step(sub, carry):
            child = lax.rem(sub // 2 ** section, 2)
            low = lax.rem(sub, 2 ** section)
            group = sub // 2 ** (section + 1) * 2 ** section + low
            for half in range(2):
                lanes = slice(half * 128, half * 128 + 128)
                taps = [weights[section, sub, j : j + 1, lanes] for j in range(WIDTH)]
                near = [fine[section, sub, c, :, lanes] for c in range(2)]
                source = image.at[sub, :, half, pl.ds(first, rows + 8), :]
                for row in range(0, rows, 16):

                    def load(part, shift):
                        return source[part, row + shift : row + shift + 16, :]

                    tile = row // 16
                    real, imag = turn_tile(
                        load,
                        taps,
                        [
                            coarse[section - 1, sub, chunk, c, tile : tile + 1, lanes]
                            for c in range(2)
                        ],
                        near,
                    )
                    target = pl.ds(pl.multiple_of(first + row, 16), 16)
                    turned[child, group, 0, target, lanes] = real.astype(BF16)
                    turned[child, group, 1, target, lanes] = imag.astype(BF16)
            return carry

        lax.fori_loop(0, GROUP, step, 0)

    def out_rows(chunk):
        return pl.ds(pl.multiple_of(me * BLOCK + place_of(chunk, UPPER2, me), 16), TURN2[chunk])

    def out_copy(chunk, k):
        return pltpu.make_async_remote_copy(
            src_ref=done.at[chunk, peers[k]],
            dst_ref=got.at[:, out_rows(chunk), :],
            send_sem=out_send.at[chunk, k],
            recv_sem=out_recv.at[chunk, k],
            device_id=(base + peers[k], rng),
            device_id_type=MESH,
        )

    def own_out_copy(chunk):
        return pltpu.make_async_copy(
            done.at[chunk, me], got.at[:, out_rows(chunk), :], own_sem.at[2 + chunk]
        )

    low_end = jnp.logical_and(rng == 0, me == 0)
    high_end = jnp.logical_and(rng == ranges - 1, me == GROUP - 1)
    image1[:, :, :, SENT : SENT + 8, :] = jnp.zeros((GROUP, 2, 2, 8, 128), F32)

    for chunk in range(2):
        for k in range(1, GROUP):
            in_copy(chunk, k, me).wait_recv()
        own_in_copy(chunk).wait()
        first, rows = in_rows(chunk, me)
        keep(0, merge(0, got0, first, rows), image1, first, rows)
        if chunk == 1:

            @pl.when(low_end)
            def _():
                image1[:, :, :, 0:8, :] = jnp.zeros((GROUP, 2, 2, 8, 128), F32)

            @pl.when(high_end)
            def _():
                image1[:, :, :, SENT - 8 : SENT, :] = jnp.zeros((GROUP, 2, 2, 8, 128), F32)

        first, rows = place_of(chunk, UPPER1, me), TURN1[chunk]
        turn(1, chunk, image1, turned1, first, rows)
        keep(1, merge(1, turned1, first, rows), image2, first, rows)
        if chunk == 1:

            @pl.when(low_end)
            def _():
                image2[:, :, :, 0:4, :] = jnp.zeros((GROUP, 2, 2, 4, 128), F32)

            @pl.when(high_end)
            def _():
                image2[:, :, :, BLOCK + 4 : BLOCK + 8, :] = jnp.zeros((GROUP, 2, 2, 4, 128), F32)

        first, rows = place_of(chunk, UPPER2, me), TURN2[chunk]
        turn(2, chunk, image2, turned2, first, rows)
        product = merge(2, turned2, first, rows)
        for group in range(4):
            for side in range(2):
                done[chunk, place(2, group, side)] = (
                    product[
                        group * 2 * rows : (group + 1) * 2 * rows,
                        side * BEAMS : (side + 1) * BEAMS,
                    ]
                    .reshape(2, rows, BEAMS)
                    .astype(BF16)
                )
        for k in order:
            out_copy(chunk, k).start()
        own_out_copy(chunk).start()

    for chunk in range(2):
        own_out_copy(chunk).wait()
        for k in range(1, GROUP):
            out_copy(chunk, k).wait_recv()
    for k in range(1, GROUP):
        for chunk in range(2):
            in_copy(chunk, k, peers[k]).wait_send()
            out_copy(chunk, k).wait_send()

    @pl.when(has_after)
    def _():
        edge_copy(0).wait_send()

    @pl.when(has_before)
    def _():
        edge_copy(1).wait_send()


def finish(got_hbm, out_hbm, got, spaced, packed, loaded, sent):
    beams = BEAMS // PIECES
    loads, copies = [], []
    for piece in range(PIECES):
        lanes = slice(piece * beams, (piece + 1) * beams)
        loads.append(
            pltpu.make_async_copy(got_hbm.at[:, :, lanes], got.at[piece], loaded.at[piece])
        )
        loads[-1].start()
    for piece in range(PIECES):
        first = piece * beams
        loads[piece].wait()
        for block in range(GROUP):
            for part in range(2):
                spaced[piece, pl.ds(2 * block + part, beams, stride=PITCH), :] = jnp.transpose(
                    got[piece, part, block * BLOCK : (block + 1) * BLOCK, :].astype(F32)
                )
        for beam in range(beams):
            start = PITCH * beam
            packed[first + beam] = spaced[piece, start : start + 2 * GROUP, :].astype(BF16)
        copies.append(
            pltpu.make_async_copy(
                packed.at[first : first + beams],
                out_hbm.at[first : first + beams],
                sent.at[piece],
            )
        )
        copies[-1].start()
    for copy in copies:
        copy.wait()


def body(subimages, taps, tap_offsets, rates, phases, band_values, band_starts):
    ranges = lax.axis_size("range")
    blocks = subimages.reshape(BEAMS, 2, GROUP, BLOCK).transpose(0, 2, 1, 3)
    blocks = blocks.reshape(BEAMS, 2 * GROUP, BLOCK)
    merged = pl.pallas_call(
        functools.partial(kernel, ranges),
        out_shape=jax.ShapeDtypeStruct((2, BINS, BEAMS), BF16),
        in_specs=[pl.BlockSpec(memory_space=pl.ANY)] * 7,
        out_specs=pl.BlockSpec(memory_space=pl.ANY),
        scratch_shapes=[
            pltpu.VMEM((BEAMS, 2 * GROUP, BLOCK), BF16),
            pltpu.VMEM((GROUP, 3, TAPS, BEAMS), F32),
            pltpu.VMEM((3, GROUP, BEAMS), jnp.int32),
            pltpu.VMEM((3, GROUP, BEAMS), F32),
            pltpu.VMEM((3, GROUP, BEAMS), F32),
            pltpu.VMEM((3, 2, BAND, 2 * BEAMS), BF16),
            pltpu.VMEM((3, 2, 2 * BEAMS), jnp.int32),
            pltpu.VMEM((BEAMS * PITCH, BLOCK), F32),
            pltpu.SemaphoreType.DMA((10,)),
            pltpu.VMEM((2, 2, BINS + 2 * EDGE, 128), F32),
            pltpu.VMEM((2, 2, EDGE, BEAMS), BF16),
            pltpu.VMEM((2, 2, EDGE, BEAMS), BF16),
            pltpu.VMEM((2, TURNED, BEAMS), BF16),
            pltpu.VMEM((2, 4, 2, SENT, BEAMS), BF16),
            pltpu.VMEM((GROUP, 2, 2, SENT + 8, 128), F32),
            pltpu.VMEM((2, 4, 2, SENT, BEAMS), BF16),
            pltpu.VMEM((GROUP, 2, 2, SENT, 128), F32),
            pltpu.VMEM((2, 4, 2, BLOCK, BEAMS), BF16),
            pltpu.VMEM((2, GROUP, 2, BLOCK // 2, BEAMS), BF16),
            pltpu.VMEM((3, 2 * BEAMS, 2 * BEAMS), BF16),
            pltpu.VMEM((3, GROUP, 16, BEAMS), F32),
            pltpu.VMEM((2, GROUP, 2, 2, 8, BEAMS), F32),
            pltpu.VMEM((3, GROUP, 2, 16, BEAMS), F32),
            pltpu.VMEM((GROUP + 1, 2, 8, BEAMS), F32),
            pltpu.SemaphoreType.REGULAR((2,)),
            pltpu.SemaphoreType.DMA((2,)),
            pltpu.SemaphoreType.DMA((2,)),
            pltpu.SemaphoreType.DMA((2, GROUP)),
            pltpu.SemaphoreType.DMA((2, GROUP)),
            pltpu.SemaphoreType.DMA((2, GROUP)),
            pltpu.SemaphoreType.DMA((2, GROUP)),
            pltpu.SemaphoreType.DMA((4,)),
        ],
        compiler_params=pltpu.CompilerParams(
            collective_id=0, has_side_effects=True, vmem_limit_bytes=58 * 2 ** 20
        ),
    )(
        blocks,
        jnp.transpose(taps, (0, 1, 3, 2)),
        jnp.transpose(tap_offsets, (1, 0, 2)),
        jnp.transpose(rates, (1, 0, 2)),
        jnp.transpose(phases, (1, 0, 2)),
        jnp.transpose(band_values, (0, 1, 3, 2)),
        band_starts,
    )
    merged = pl.pallas_call(
        finish,
        out_shape=jax.ShapeDtypeStruct((BEAMS, 2 * GROUP, BLOCK), BF16),
        in_specs=[pl.BlockSpec(memory_space=pl.ANY)],
        out_specs=pl.BlockSpec(memory_space=pl.ANY),
        scratch_shapes=[
            pltpu.VMEM((PIECES, 2, BINS, BEAMS // PIECES), BF16),
            pltpu.VMEM((PIECES, BEAMS // PIECES * PITCH, BLOCK), F32),
            pltpu.VMEM((BEAMS, 2 * GROUP, BLOCK), BF16),
            pltpu.SemaphoreType.DMA((PIECES,)),
            pltpu.SemaphoreType.DMA((PIECES,)),
        ],
        compiler_params=pltpu.CompilerParams(vmem_limit_bytes=58 * 2 ** 20),
    )(merged)
    merged = merged.reshape(BEAMS, GROUP, 2, BLOCK).transpose(0, 2, 1, 3)
    return merged.reshape(1, BEAMS, 2, BINS)


def solution(mesh):
    placed = (P("pulse", None, None, "range"), P(), P(), P(), P(), P(), P())
    return jax.shard_map(
        body, mesh=mesh, in_specs=placed, out_specs=P("pulse", None, None, "range"), check_vma=False
    )
```
